32 devices in a mesh: pair: 8 (over z, core), aux: 4 (over y, x).
Axes of the slice: x: 2, y: 2, z: 4, core: 2. Of those that a mesh axis runs over, the one named last changes fastest.
Arguments:
- c_occ: bfloat16 [12288, 1024], P('pair', 'aux'), may hold values from -0.1875 to 0.1875
- c_vir: bfloat16 [12288, 11264], P('pair', 'aux'), may hold values from -0.0546875 to 0.0546875
- e_occ: float32 [1024], P('aux'), may hold values from -2 to -0.3
- e_vir: float32 [11264], P('aux'), may hold values from 0.2 to 3
- tau_points: float32 [2], replicated, may hold values from 0.2 to 2
- pair_blocks: int32 [32, 2], P('pair'), may hold values from 0 to 767
- block_count: int32 [8], P('pair'), may hold values from 1 to 4, 20 in all
- three_center: bfloat16 [9216, 32, 256], P('aux', 'pair'), may hold values from -0.59765625 to 0.59765625
Outputs:
- coupling: float32 [9216, 2, 512], P(('aux', 'pair'))
The draws below stay inside these ranges and needn't reach their ends.
Inputs may be any that keep to these rules, and one draw needn't show every extreme that they name: pair_blocks[s] names the AO shell blocks of the rows and the columns of slot s. Slots s with s mod 4 < block_count[s // 4] are live, the others are ignored; some index of pair has all 4 slots live.
All inputs are finite; a program needn't handle non-finite values. No bound on the sum of `block_count` on one device may be relied on, other than what follows from the above.
Results may differ from the reference program's by a relative error of at most 0.0046.
Values may be sent and summed in bfloat16 or wider, within the bound.
A program may use at most 128 MiB of HBM per device.

```python
import math
import jax
import jax.numpy as jnp
import numpy as np
from jax import lax

BS = 16
NAO = 12288
NOCC = 1024
NVIR = 11264
AUX_DEV = 2304
K_DEV = 4
TAUS = 2
WIN_DEV = 128
NAUX = 9216
WIN = 512
NBLK = 768
TOTAL_BLK = 32
N_PAIR = 8
N_AUX = 4


def touch_ends(result, own_key, least, largest):
    place = [jax.random.randint(jax.random.fold_in(own_key, axis), (), 0, length) for axis, length in enumerate(result.shape)]
    widest = result.shape.index(max(result.shape))
    next_to = place[:widest] + [(place[widest] + 1) % result.shape[widest]] + place[widest + 1:]
    return result.at[tuple(place)].set(least).at[tuple(next_to)].set(largest)


def raised(values, own_key, source, target, parts, factor):
    owner, partner = [(jnp.arange(values.shape[axis_at]) // (values.shape[axis_at] // parts)).reshape([-1 if axis == axis_at else 1 for axis in range(values.ndim)]) for axis_at in (source, target)]
    chosen = jax.random.permutation(own_key, parts)[partner]
    strong = (owner == chosen) | (owner == (partner + parts // 2) % parts)
    return jnp.where(strong, factor * values, values)


def level_of(rng, dims, split, low, high):
    def one(position, parts):
        heights = jax.random.uniform(jax.random.fold_in(jax.random.fold_in(rng, 6), position), (parts,), jnp.float32, low / len(split), high / len(split))
        return jnp.repeat(jnp.exp(heights), dims[position] // parts).reshape((-1,) + (1,) * (len(dims) - position - 1))

    gain = one(*split[0])
    for cut in split[1:]:
        gain = gain * one(*cut)
    return gain


def profile(count, total, bound, slope):
    portions = [(1 << 20) // math.isqrt(rank ** slope) + 1 for rank in range(2, count + 1)]
    surplus, given = total - bound - (count - 1), [1] * (count - 1)
    while surplus > 0:
        free = [i for i in range(count - 1) if given[i] < bound]
        whole, budget = sum([portions[i] for i in free]), surplus
        for i in free:
            extra = min(bound - given[i], max(1, budget * portions[i] // whole), surplus)
            given[i] = given[i] + extra
            surplus = surplus - extra
    return np.array([bound] + given)


def ragged_sizes(stream_key, count, total, bound, skew):
    if count == 2:
        one = jax.random.randint(stream_key, (), max(1, total - bound), min(bound, total - 1) + 1)
        return jnp.stack([one, total - one])
    sizes = jnp.asarray(profile(count, total, bound, skew), jnp.int32)
    couples = (count - 1) // 2
    giver, receiver = sizes[1:1 + 2 * couples:2], sizes[2:2 + 2 * couples:2]
    slack = jnp.minimum(giver - 1, bound - receiver)
    passed = jax.random.randint(jax.random.fold_in(stream_key, 1), (couples,), 0, 1 << 20) % (slack + 1)
    sizes = sizes.at[1:1 + 2 * couples:2].set(giver - passed).at[2:2 + 2 * couples:2].set(receiver + passed)
    return sizes[jax.random.permutation(jax.random.fold_in(stream_key, 2), count)]


def scatter_about(stream_key, shape, spread, most, shards=(), kind=jnp.bfloat16):
    entries = spread * jax.random.normal(stream_key, shape, jnp.float32)
    if shards:
        entries = entries * level_of(stream_key, shape, shards, -0.22, 0.18)
    return jnp.clip(entries, -most, most).astype(kind)


def noise_with(key, extent, spread, reach, cuts, heavy, held_as=jnp.bfloat16):
    result = spread * jax.random.normal(key, extent, jnp.float32)
    if cuts:
        result = result * level_of(key, extent, cuts, -0.22, 0.18)
    return jnp.clip(raised(result, jax.random.fold_in(key, 3), *heavy), -reach, reach).astype(held_as)


def setup_inputs(seed: int = 0) -> dict:
    keys = jax.random.split(jax.random.key(seed), 9)
    return {
        "c_occ": scatter_about(keys[0], (NAO, NOCC), NOCC ** -0.5, 0.1875, ((0, 8), (1, 4))),
        "c_vir": scatter_about(keys[1], (NAO, NVIR), NVIR ** -0.5, 0.0546875, ((0, 8), (1, 4))),
        "e_occ": jnp.clip(-2.0 + 1.7 * jax.random.uniform(keys[2], (NOCC,), jnp.float32) ** level_of(keys[2], (NOCC,), ((0, 4),), -0.2, 0.2), -2.0, -0.3),
        "e_vir": jnp.clip(0.2 + 2.8 * jax.random.uniform(keys[3], (NVIR,), jnp.float32) ** level_of(keys[3], (NVIR,), ((0, 4),), -0.2, 0.2), 0.2, 3.0),
        "tau_points": jnp.clip(jnp.exp(jax.random.uniform(keys[4], (TAUS,), jnp.float32, math.log(0.2), math.log(2.0))), 0.2, 2.0),
        "pair_blocks": touch_ends(jax.random.randint(keys[5], (TOTAL_BLK, 2), 0, NBLK), jax.random.fold_in(keys[5], 1), 0, NBLK - 1).astype(jnp.int32),
        "block_count": ragged_sizes(keys[6], N_PAIR, 5 * N_PAIR // 2, K_DEV, 2).astype(jnp.int32),
        "three_center": noise_with(keys[7], (NAUX, TOTAL_BLK, BS * BS), 0.1, 0.59765625, ((0, 4), (1, 8)), (1, 0, 8, 2.0)),
    }


def slot_rows(coefficient, energy, exponent_sign, tau_value, names):
    factor = jnp.exp(exponent_sign * tau_value * energy / 2.0)
    scaled = (coefficient.astype(jnp.float32) * factor[None, :]).astype(jnp.bfloat16)
    scaled = lax.optimization_barrier(scaled)
    blocks = scaled.reshape(NAO // BS, BS, coefficient.shape[1])
    return blocks[names].astype(jnp.float32)


def cross_tiles(rows):
    return jnp.einsum('sin,rjn->srij', rows, rows).astype(jnp.bfloat16)


def reference(c_occ, c_vir, e_occ, e_vir, tau_points, pair_blocks, block_count, three_center):
    occ_tiles = jnp.stack([cross_tiles(slot_rows(c_occ, e_occ, 1.0, tau_points[step], pair_blocks[:, 0])) for step in range(TAUS)])
    vir_tiles = jnp.stack([cross_tiles(slot_rows(c_vir, e_vir, -1.0, tau_points[step], pair_blocks[:, 1])) for step in range(TAUS)])
    slot_ids = jnp.arange(TOTAL_BLK, dtype=jnp.int32)
    live_mask = (slot_ids % K_DEV < block_count[slot_ids // K_DEV]).astype(jnp.float32)
    window = three_center.reshape(N_AUX, AUX_DEV, TOTAL_BLK, BS * BS)[:, :WIN_DEV]
    window = window.reshape(WIN, TOTAL_BLK, BS, BS).astype(jnp.float32)
    window = window * live_mask[None, :, None, None]
    occ_float = occ_tiles.astype(jnp.float32)
    vir_float = vir_tiles.astype(jnp.float32)

    def one_target(target):
        target = jnp.asarray(target).astype(jnp.int32)
        occ_row = lax.dynamic_index_in_dim(occ_float, target, 1, keepdims=False)
        vir_row = lax.dynamic_index_in_dim(vir_float, target, 1, keepdims=False)
        half_moved = jnp.einsum('tsij,psjl->tpsil', occ_row, window).astype(jnp.bfloat16)
        half_moved = lax.optimization_barrier(half_moved)
        summed = jnp.einsum('tpsil,tsml->tpim', half_moved.astype(jnp.float32), vir_row)
        summed = summed * lax.dynamic_index_in_dim(live_mask, target, 0, keepdims=False)
        return summed.astype(jnp.bfloat16).reshape(TAUS, WIN, BS * BS)

    moved = lax.map(one_target, slot_ids)
    moved = moved.reshape(N_PAIR, K_DEV, TAUS, WIN, BS * BS)

    def add_group(group, running):
        group = jnp.asarray(group).astype(jnp.int32)
        group_blocks = lax.dynamic_slice_in_dim(three_center, (group * K_DEV).astype(jnp.int32), K_DEV, 1)
        group_blocks = group_blocks.reshape(NAUX, K_DEV * BS * BS)
        right_side = lax.dynamic_index_in_dim(moved, group, 0, keepdims=False)
        right_side = right_side.transpose(1, 2, 0, 3).reshape(TAUS * WIN, K_DEV * BS * BS)
        return running + jnp.dot(group_blocks, right_side.T, preferred_element_type=jnp.float32)

    running = lax.fori_loop(0, N_PAIR, add_group, jnp.zeros((NAUX, TAUS * WIN), jnp.float32))
    return running.reshape(NAUX, TAUS, WIN)
```

```python
import functools

import jax
import jax.numpy as jnp
from jax import lax
from jax.experimental import pallas as pl
from jax.experimental.pallas import tpu as pltpu
from jax.sharding import PartitionSpec as P

BS = 16
TAUS = 2
WIN_DEV = 128
MESH = pl.DeviceIdType.MESH
VMEM = pl.BlockSpec(memory_space=pltpu.VMEM)
DMA = pltpu.SemaphoreType.DMA
BF16 = jnp.bfloat16
F32 = jnp.float32


def params(collective_id):
    return pltpu.CompilerParams(
        collective_id=collective_id, has_side_effects=True, vmem_limit_bytes=40 * 2**20
    )


def greet(pair_peers, aux_peers=()):
    barrier = pltpu.get_barrier_semaphore()
    for peer in pair_peers:
        pl.semaphore_signal(barrier, inc=1, device_id={"pair": peer}, device_id_type=MESH)
    for peer in aux_peers:
        pl.semaphore_signal(barrier, inc=1, device_id={"aux": peer}, device_id_type=MESH)
    pl.semaphore_wait(barrier, len(pair_peers) + len(aux_peers))


def remote(source, target, send, received, axis, device):
    return pltpu.make_async_remote_copy(
        src_ref=source,
        dst_ref=target,
        send_sem=send,
        recv_sem=received,
        device_id={axis: device},
        device_id_type=MESH,
    )


def place():
    me = lax.axis_index("pair")
    core = lax.rem(me, 2)
    return me, core, me // 2, me + 1 - 2 * core


def table_kernel(groups, mine, out, send, received):
    me = lax.axis_index("pair")
    peers = [lax.rem(me + k, groups) for k in range(1, groups)]
    greet(peers)
    copies = []
    for k in range(groups - 1):
        copy = remote(mine, out.at[me], send.at[k], received.at[k], "pair", peers[k])
        copy.start()
        copies.append(copy)
    out[me] = mine[...]
    for copy in copies:
        copy.wait()


def gather_table(table, groups):
    return pl.pallas_call(
        functools.partial(table_kernel, groups),
        out_shape=jax.ShapeDtypeStruct((groups,) + table.shape, table.dtype),
        in_specs=[VMEM],
        out_specs=VMEM,
        scratch_shapes=[DMA((groups - 1,)), DMA((groups - 1,))],
        compiler_params=params(0),
    )(table)


def rows_kernel(chips, chunks, rows, out, own, right_in, left_in, right_out, left_out,
                own_send, own_recv, right_send, right_recv, left_send, left_recv,
                done_send, done_recv):
    me, core, chip, partner = place()
    last = chips - 1
    after = lax.rem(me + 2, 2 * chips)
    before = lax.rem(me + 2 * chips - 2, 2 * chips)
    greet([partner, after, before])

    def swap(j):
        return remote(rows.at[1 - core, j], own.at[j], own_send.at[j], own_recv.at[j], "pair", partner)

    def rightward(j):
        return remote(right_out.at[j], right_in.at[j], right_send.at[j], right_recv.at[j], "pair", after)

    def leftward(j):
        return remote(left_out.at[j], left_in.at[j], left_send.at[j], left_recv.at[j], "pair", before)

    def finished(j):
        return remote(out.at[core, j], out.at[core, j], done_send.at[j], done_recv.at[j], "pair", partner)

    def start_swap(j, carry):
        swap(j).start()
        return carry

    lax.fori_loop(0, chunks, start_swap, 0)

    def step(i, carry):
        @pl.when(i < chunks)
        def _():
            swap(i).wait_recv()
            own[i] = own[i] + rows[core, i]

        to_right = i - chip

        @pl.when((to_right >= 0) & (to_right < chunks))
        def _():
            @pl.when(chip > 0)
            def _():
                rightward(to_right).wait_recv()

            @pl.when(chip == 0)
            def _():
                right_out[to_right] = own[to_right]

            @pl.when((chip > 0) & (chip < last))
            def _():
                right_out[to_right] = own[to_right] + right_in[to_right]

            @pl.when(chip < last)
            def _():
                rightward(to_right).start()

        to_left = i - (last - chip)

        @pl.when((to_left >= 0) & (to_left < chunks))
        def _():
            @pl.when(chip < last)
            def _():
                leftward(to_left).wait_recv()

            @pl.when(chip == last)
            def _():
                left_out[to_left] = own[to_left]

            @pl.when((chip > 0) & (chip < last))
            def _():
                left_out[to_left] = own[to_left] + left_in[to_left]

            @pl.when(chip > 0)
            def _():
                leftward(to_left).start()

        ready = i - jnp.maximum(chip, last - chip)

        @pl.when((ready >= 0) & (ready < chunks))
        def _():
            @pl.when(chip == 0)
            def _():
                out[core, ready] = own[ready] + left_in[ready]

            @pl.when(chip == last)
            def _():
                out[core, ready] = own[ready] + right_in[ready]

            @pl.when((chip > 0) & (chip < last))
            def _():
                out[core, ready] = own[ready] + left_in[ready] + right_in[ready]

            finished(ready).start()

        return carry

    lax.fori_loop(0, chunks + last, step, 0)

    def drain(j, carry):
        swap(j).wait_send()

        @pl.when(chip < last)
        def _():
            rightward(j).wait_send()

        @pl.when(chip > 0)
        def _():
            leftward(j).wait_send()

        finished(j).wait_send()
        remote(
            out.at[1 - core, j], out.at[1 - core, j], done_send.at[j], done_recv.at[j], "pair", partner
        ).wait_recv()
        return carry

    lax.fori_loop(0, chunks, drain, 0)


def sum_rows(rows, groups):
    chunks = rows.shape[0] // (2 * BS)
    width = rows.shape[1]
    shape = (2, chunks, BS, width)
    summed = pl.pallas_call(
        functools.partial(rows_kernel, groups // 2, chunks),
        out_shape=jax.ShapeDtypeStruct(shape, rows.dtype),
        in_specs=[VMEM],
        out_specs=VMEM,
        scratch_shapes=[pltpu.VMEM(shape[1:], rows.dtype)] * 5 + [DMA((chunks,))] * 8,
        compiler_params=params(1),
    )(rows.reshape(shape))
    return summed.reshape(rows.shape)


def tiles_kernel(shards, chips, terms, window, tiles, blocks, held,
                 term_send, term_recv, tile_send, tile_recv,
                 far_send, far_recv, near_send, near_recv):
    me, core, chip, partner = place()
    shard = lax.axis_index("aux")
    peers = [lax.rem(shard + k, shards) for k in range(1, shards)]
    line = [lax.rem(chip + k, chips) * 2 + core for k in range(1, chips)]
    greet([partner] + line, peers)
    parts = []
    for k, peer in enumerate(peers):
        copy = remote(terms.at[peer], held.at[k], term_send.at[k], term_recv.at[k], "aux", peer)
        copy.start()
        parts.append(copy)
    far = []
    for k, peer in enumerate(line):
        copy = remote(window, blocks.at[me], far_send.at[k], far_recv.at[k], "pair", peer)
        copy.start()
        far.append(copy)
    near = [remote(window, blocks.at[me], near_send.at[0], near_recv.at[0], "pair", partner)]
    near[0].start()
    blocks[me] = window[...]
    total = terms[shard]
    for k, copy in enumerate(parts):
        copy.wait_recv()
        total = total + held[k]
    tiles[shard] = total.astype(tiles.dtype)
    sums = []
    for k, peer in enumerate(peers):
        copy = remote(tiles.at[shard], tiles.at[shard], tile_send.at[k], tile_recv.at[k], "aux", peer)
        copy.start()
        sums.append(copy)
    for k, copy in enumerate(far):
        copy.wait_recv()
        origin = lax.rem(chip + chips - 1 - k, chips) * 2 + core
        pass_on = remote(
            blocks.at[origin], blocks.at[origin], near_send.at[k + 1], near_recv.at[k + 1], "pair", partner
        )
        pass_on.start()
        near.append(pass_on)
    for copy in sums + near:
        copy.wait()
    for copy in parts + far:
        copy.wait_send()


def sum_tiles(terms, window, shards, groups):
    chips = groups // 2
    rows, width = terms.shape
    grouped = (shards, rows // shards, width)
    sems = [DMA((shards - 1,))] * 4 + [DMA((chips - 1,))] * 2 + [DMA((chips,))] * 2
    tiles, blocks = pl.pallas_call(
        functools.partial(tiles_kernel, shards, chips),
        out_shape=(
            jax.ShapeDtypeStruct(grouped, BF16),
            jax.ShapeDtypeStruct((groups,) + window.shape, BF16),
        ),
        in_specs=[VMEM, VMEM],
        out_specs=(VMEM, VMEM),
        scratch_shapes=[pltpu.VMEM((shards - 1,) + grouped[1:], F32)] + sems,
        compiler_params=params(2),
    )(terms.reshape(grouped), window)
    return tiles.reshape(rows, width), blocks


def moved_kernel(shards, mine, out, send, received):
    shard = lax.axis_index("aux")
    peers = [lax.rem(shard + k, shards) for k in range(1, shards)]
    greet([], peers)
    copies = []
    for t in range(TAUS):
        for k, peer in enumerate(peers):
            at = t * (shards - 1) + k
            copy = remote(mine.at[t], out.at[t, shard], send.at[at], received.at[at], "aux", peer)
            copy.start()
            copies.append(copy)
    for t in range(TAUS):
        out[t, shard] = mine[t]
    for copy in copies:
        copy.wait()


def gather_moved(moved, shards):
    count = TAUS * (shards - 1)
    return pl.pallas_call(
        functools.partial(moved_kernel, shards),
        out_shape=jax.ShapeDtypeStruct((TAUS, shards) + moved.shape[1:], moved.dtype),
        in_specs=[VMEM],
        out_specs=VMEM,
        scratch_shapes=[DMA((count,)), DMA((count,))],
        compiler_params=params(3),
    )(moved)


def coupling_kernel(chips, terms, out, near, leaving, arriving,
                    near_send, near_recv, far_send, far_recv):
    me, core, chip, partner = place()
    line = [lax.rem(chip + k, chips) for k in range(1, chips)]
    greet([partner] + [z * 2 + core for z in line])
    order = line + [chip]
    swaps = []
    for k, z in enumerate(order):
        copy = remote(terms.at[z, 1 - core], near.at[k], near_send.at[k], near_recv.at[k], "pair", partner)
        copy.start()
        swaps.append(copy)
    sent = []
    for k, z in enumerate(line):
        swaps[k].wait_recv()
        leaving[k] = (terms[z, core].astype(F32) + near[k].astype(F32)).astype(leaving.dtype)
        copy = remote(
            leaving.at[k], arriving.at[k], far_send.at[k], far_recv.at[k], "pair", z * 2 + core
        )
        copy.start()
        sent.append(copy)
    swaps[-1].wait_recv()
    out[...] = terms[chip, core].astype(F32) + near[chips - 1].astype(F32)
    for k, copy in enumerate(sent):
        copy.wait_recv()
        out[...] += arriving[k].astype(F32)
    for copy in swaps + sent:
        copy.wait_send()


def sum_coupling(terms, groups):
    chips = groups // 2
    rows, width = terms.shape
    block = (rows // groups, width)
    return pl.pallas_call(
        functools.partial(coupling_kernel, chips),
        out_shape=jax.ShapeDtypeStruct(block, F32),
        in_specs=[VMEM],
        out_specs=VMEM,
        scratch_shapes=[
            pltpu.VMEM((chips,) + block, terms.dtype),
            pltpu.VMEM((chips - 1,) + block, terms.dtype),
            pltpu.VMEM((chips - 1,) + block, terms.dtype),
        ]
        + [DMA((chips,))] * 2
        + [DMA((chips - 1,))] * 2,
        compiler_params=params(4),
    )(terms.reshape((chips, 2) + block))


def owned_rows(coefficient, names, group):
    local_blocks = coefficient.shape[0] // BS
    blocks = coefficient.reshape(local_blocks, BS, coefficient.shape[1])
    local_names = names - group * local_blocks
    owned = (local_names >= 0) & (local_names < local_blocks)
    picked = jnp.take(blocks, jnp.clip(local_names, 0, local_blocks - 1), axis=0)
    picked = jnp.where(owned[:, None, None], picked, jnp.zeros((), BF16))
    return picked.reshape(names.shape[0] * BS, coefficient.shape[1])


def own_gram(rows, energy, exponent_sign, tau_points, picks):
    factor = jnp.exp(exponent_sign * tau_points[:, None] * energy[None, :] / 2.0)
    scaled = (rows[None].astype(F32) * factor[:, None, :]).astype(BF16)
    own = jnp.concatenate(
        [lax.dynamic_slice_in_dim(scaled, pick * BS, BS, 1) for pick in picks], axis=1
    )
    return jnp.einsum("tin,tjn->tij", own, scaled, preferred_element_type=F32)


def per_device(groups, shards, c_occ, c_vir, e_occ, e_vir, tau_points, pair_blocks, block_count,
               three_center):
    own_slots = pair_blocks.shape[0]
    slot_total = own_slots * groups
    live_total = 5 * groups // 2
    group = lax.axis_index("pair")
    fields = 2 * own_slots + 1
    flat = jnp.concatenate([pair_blocks.reshape(-1), block_count])
    table = jnp.zeros((8, 128), jnp.int32).at[0, :fields].set(flat)
    tables = gather_table(table, groups)[:, 0, :fields]
    names = tables[:, :-1].reshape(slot_total, 2)
    counts = tables[:, -1]
    live = (jnp.arange(own_slots)[None, :] < counts[:, None]).reshape(slot_total)
    ids = jnp.arange(slot_total)
    ranks = jnp.sum(jnp.where(live[None, :] & (ids[None, :] < ids[:, None]), 1, 0), axis=1)
    select = live[None, :] & (ranks[None, :] == jnp.arange(live_total)[:, None])
    live_names = jnp.sum(jnp.where(select[:, :, None], names[None], 0), axis=1)
    rows = jnp.concatenate(
        [owned_rows(c_occ, live_names[:, 0], group), owned_rows(c_vir, live_names[:, 1], group)], axis=1
    )
    rows = sum_rows(rows, groups)
    before = jnp.sum(jnp.where(jnp.arange(groups) < group, counts, 0))
    picks = [jnp.minimum(before + k, live_total - 1) for k in range(own_slots)]
    n_occ = c_occ.shape[1]
    terms = jnp.concatenate(
        [
            own_gram(rows[:, :n_occ], e_occ, 1.0, tau_points, picks),
            own_gram(rows[:, n_occ:], e_vir, -1.0, tau_points, picks),
        ],
        axis=0,
    )
    flat_blocks = three_center.reshape(three_center.shape[0], own_slots * BS * BS)
    tiles, window = sum_tiles(
        terms.reshape(2 * TAUS * own_slots * BS, live_total * BS), flat_blocks[:WIN_DEV], shards, groups
    )
    spread = (
        select[:, None, :, None] & jnp.eye(BS, dtype=bool)[None, :, None, :]
    ).astype(BF16).reshape(live_total * BS, slot_total * BS)
    tiles = jnp.dot(tiles, spread, preferred_element_type=F32).astype(BF16)
    tiles = tiles.reshape(2, TAUS, own_slots, BS, slot_total, BS)
    occ_tiles, vir_tiles = tiles[0], tiles[1]
    blocks = window.reshape(groups, WIN_DEV, own_slots, BS, BS).transpose(1, 0, 2, 3, 4)
    blocks = blocks.reshape(WIN_DEV, slot_total, BS, BS)
    half_moved = jnp.einsum(
        "tkisj,psjl->tpksil", occ_tiles, blocks, preferred_element_type=F32
    ).astype(BF16)
    moved = jnp.einsum("tpksil,tkmsl->tpkim", half_moved, vir_tiles, preferred_element_type=F32)
    live_mask = jnp.arange(own_slots) < block_count[0]
    moved = moved * live_mask.astype(F32)[None, None, :, None, None]
    transformed = moved.astype(BF16).reshape(TAUS, WIN_DEV, own_slots * BS * BS)
    everyone = gather_moved(transformed, shards)
    everyone = everyone.reshape(TAUS * shards * WIN_DEV, own_slots * BS * BS)
    partials = lax.dot_general(
        flat_blocks, everyone, (((1,), (1,)), ((), ())), preferred_element_type=F32
    ).astype(BF16)
    coupling = sum_coupling(partials, groups)
    return coupling.reshape(coupling.shape[0], TAUS, shards * WIN_DEV)


def solution(mesh):
    placed = (
        P("pair", "aux"),
        P("pair", "aux"),
        P("aux"),
        P("aux"),
        P(),
        P("pair", None),
        P("pair"),
        P("aux", "pair", None),
    )
    return jax.shard_map(
        functools.partial(per_device, mesh.shape["pair"], mesh.shape["aux"]),
        mesh=mesh,
        in_specs=placed,
        out_specs=P(("aux", "pair"), None, None),
        check_vma=False,
    )
```

```python
import functools

import jax
import jax.numpy as jnp
from jax import lax
from jax.experimental import pallas as pl
from jax.experimental.pallas import tpu as pltpu
from jax.sharding import PartitionSpec as P

BS = 16
TAUS = 2
WIN_DEV = 128
HOP = 2
MESH = pl.DeviceIdType.MESH
VMEM = pl.BlockSpec(memory_space=pltpu.VMEM)
DMA = pltpu.SemaphoreType.DMA
BF16 = jnp.bfloat16
F32 = jnp.float32


def params(collective_id):
    return pltpu.CompilerParams(
        collective_id=collective_id, has_side_effects=True, vmem_limit_bytes=40 * 2**20
    )


def greet(pair_peers, aux_peers=()):
    barrier = pltpu.get_barrier_semaphore()
    for peer in pair_peers:
        pl.semaphore_signal(barrier, inc=1, device_id={"pair": peer}, device_id_type=MESH)
    for peer in aux_peers:
        pl.semaphore_signal(barrier, inc=1, device_id={"aux": peer}, device_id_type=MESH)
    pl.semaphore_wait(barrier, len(pair_peers) + len(aux_peers))


def remote(source, target, send, received, axis, device):
    return pltpu.make_async_remote_copy(
        src_ref=source,
        dst_ref=target,
        send_sem=send,
        recv_sem=received,
        device_id={axis: device},
        device_id_type=MESH,
    )


def place():
    me = lax.axis_index("pair")
    core = lax.rem(me, 2)
    return me, core, me // 2, me + 1 - 2 * core


def table_kernel(groups, mine, out, send, received):
    me = lax.axis_index("pair")
    peers = [lax.rem(me + k, groups) for k in range(1, groups)]
    greet(peers)
    copies = []
    for k in range(groups - 1):
        copy = remote(mine, out.at[me], send.at[k], received.at[k], "pair", peers[k])
        copy.start()
        copies.append(copy)
    out[me] = mine[...]
    for copy in copies:
        copy.wait()


def gather_table(table, groups):
    return pl.pallas_call(
        functools.partial(table_kernel, groups),
        out_shape=jax.ShapeDtypeStruct((groups,) + table.shape, table.dtype),
        in_specs=[VMEM],
        out_specs=VMEM,
        scratch_shapes=[DMA((groups - 1,)), DMA((groups - 1,))],
        compiler_params=params(0),
    )(table)


def rows_kernel(chips, chunks, rows, window, out, blocks,
                own, right_in, left_in, right_out, left_out,
                own_send, own_recv, right_send, right_recv, left_send, left_recv,
                done_send, done_recv, far_send, far_recv, near_send, near_recv):
    me, core, chip, partner = place()
    last = chips - 1
    after = lax.rem(me + 2, 2 * chips)
    before = lax.rem(me + 2 * chips - 2, 2 * chips)
    line = [lax.rem(chip + k, chips) * 2 + core for k in range(1, chips)]
    greet([partner] + line)

    def swap(j):
        return remote(rows.at[1 - core, j], own.at[j], own_send.at[j], own_recv.at[j], "pair", partner)

    def rightward(j):
        return remote(right_out.at[j], right_in.at[j], right_send.at[j], right_recv.at[j], "pair", after)

    def leftward(j):
        return remote(left_out.at[j], left_in.at[j], left_send.at[j], left_recv.at[j], "pair", before)

    def finished(j):
        return remote(out.at[core, j], out.at[core, j], done_send.at[j], done_recv.at[j], "pair", partner)

    def start_swap(j, carry):
        swap(j).start()
        return carry

    lax.fori_loop(0, chunks, start_swap, 0)
    far = []
    for k, peer in enumerate(line):
        far.append(remote(window, blocks.at[me], far_send.at[k], far_recv.at[k], "pair", peer))
    near = [remote(window, blocks.at[me], near_send.at[0], near_recv.at[0], "pair", partner)]
    near[0].start()
    blocks[me] = window[...]

    def step(i, carry):
        @pl.when(i < chunks)
        def _():
            swap(i).wait_recv()
            own[i] = own[i] + rows[core, i]

        to_right = i - HOP * chip

        @pl.when((to_right >= 0) & (to_right < chunks))
        def _():
            @pl.when(chip > 0)
            def _():
                rightward(to_right).wait_recv()

            @pl.when(chip == 0)
            def _():
                right_out[to_right] = own[to_right]

            @pl.when((chip > 0) & (chip < last))
            def _():
                right_out[to_right] = own[to_right] + right_in[to_right]

            @pl.when(chip < last)
            def _():
                rightward(to_right).start()

        to_left = i - HOP * (last - chip)

        @pl.when((to_left >= 0) & (to_left < chunks))
        def _():
            @pl.when(chip < last)
            def _():
                leftward(to_left).wait_recv()

            @pl.when(chip == last)
            def _():
                left_out[to_left] = own[to_left]

            @pl.when((chip > 0) & (chip < last))
            def _():
                left_out[to_left] = own[to_left] + left_in[to_left]

            @pl.when(chip > 0)
            def _():
                leftward(to_left).start()

        ready = i - HOP * jnp.maximum(chip, last - chip)

        @pl.when((ready >= 0) & (ready < chunks))
        def _():
            @pl.when(chip == 0)
            def _():
                out[core, ready] = own[ready] + left_in[ready]

            @pl.when(chip == last)
            def _():
                out[core, ready] = own[ready] + right_in[ready]

            @pl.when((chip > 0) & (chip < last))
            def _():
                out[core, ready] = own[ready] + left_in[ready] + right_in[ready]

            finished(ready).start()

        return carry

    lax.fori_loop(0, HOP * last, step, 0)
    for copy in far:
        copy.start()
    lax.fori_loop(HOP * last, chunks + HOP * last, step, 0)
    for k, copy in enumerate(far):
        copy.wait_recv()
        origin = lax.rem(chip + last - k, chips) * 2 + core
        pass_on = remote(
            blocks.at[origin], blocks.at[origin], near_send.at[k + 1], near_recv.at[k + 1], "pair", partner
        )
        pass_on.start()
        near.append(pass_on)

    def drain(j, carry):
        swap(j).wait_send()

        @pl.when(chip < last)
        def _():
            rightward(j).wait_send()

        @pl.when(chip > 0)
        def _():
            leftward(j).wait_send()

        finished(j).wait_send()
        remote(
            out.at[1 - core, j], out.at[1 - core, j], done_send.at[j], done_recv.at[j], "pair", partner
        ).wait_recv()
        return carry

    lax.fori_loop(0, chunks, drain, 0)
    for copy in near:
        copy.wait()
    for copy in far:
        copy.wait_send()


def sum_rows(rows, window, groups):
    chunks = rows.shape[0] // (2 * BS)
    width = rows.shape[1]
    shape = (2, chunks, BS, width)
    chips = groups // 2
    summed, blocks = pl.pallas_call(
        functools.partial(rows_kernel, chips, chunks),
        out_shape=(
            jax.ShapeDtypeStruct(shape, rows.dtype),
            jax.ShapeDtypeStruct((groups,) + window.shape, window.dtype),
        ),
        in_specs=[VMEM, VMEM],
        out_specs=(VMEM, VMEM),
        scratch_shapes=[pltpu.VMEM(shape[1:], rows.dtype)] * 5
        + [DMA((chunks,))] * 8
        + [DMA((chips - 1,))] * 2
        + [DMA((chips,))] * 2,
        compiler_params=params(1),
    )(rows.reshape(shape), window)
    return summed.reshape(rows.shape), blocks


def tiles_kernel(shards, terms, tiles, held, term_send, term_recv, tile_send, tile_recv):
    shard = lax.axis_index("aux")
    peers = [flipped(shard, k, shards) for k in range(1, shards)]
    greet([], peers)
    parts = []
    for k, peer in enumerate(peers):
        copy = remote(terms.at[peer], held.at[k], term_send.at[k], term_recv.at[k], "aux", peer)
        copy.start()
        parts.append(copy)
    total = terms[shard]
    for k, copy in enumerate(parts):
        copy.wait_recv()
        total = total + held[k]
    tiles[shard] = total.astype(tiles.dtype)
    sums = []
    for k, peer in enumerate(peers):
        copy = remote(tiles.at[shard], tiles.at[shard], tile_send.at[k], tile_recv.at[k], "aux", peer)
        copy.start()
        sums.append(copy)
    for copy in sums:
        copy.wait()
    for copy in parts:
        copy.wait_send()


def sum_tiles(terms, shards):
    rows, width = terms.shape
    grouped = (shards, rows // shards, width)
    tiles = pl.pallas_call(
        functools.partial(tiles_kernel, shards),
        out_shape=jax.ShapeDtypeStruct(grouped, BF16),
        in_specs=[VMEM],
        out_specs=VMEM,
        scratch_shapes=[pltpu.VMEM((shards - 1,) + grouped[1:], F32)] + [DMA((shards - 1,))] * 4,
        compiler_params=params(2),
    )(terms.reshape(grouped))
    return tiles.reshape(rows, width)


def flipped(shard, k, shards):
    other, bit = 0, 1
    while bit < shards:
        other = other + lax.rem(shard // bit + k // bit, 2) * bit
        bit = bit * 2
    return other


def coupling_kernel(chips, shards, blocks, mine, out, kept, moved, near_out, near_in, leaving, arriving,
                    moved_send, moved_recv, near_send, near_recv, far_send, far_recv):
    me, core, chip, partner = place()
    shard = lax.axis_index("aux")
    last = chips - 1
    peers = [flipped(shard, k, shards) for k in range(1, shards)]
    greet([partner] + [lax.rem(chip + k, chips) * 2 + core for k in range(1, chips)], peers)

    def arrival(k):
        return remote(
            mine, moved.at[k], moved_send.at[k], moved_recv.at[k], "aux", flipped(shard, k, shards)
        )

    def target(j):
        return lax.rem(chip + 1 + j, chips)

    def swap(k, j):
        return remote(
            near_out.at[k, j], near_in.at[k, j], near_send.at[k, j], near_recv.at[k, j], "pair", partner
        )

    def hand_over(k, j):
        return remote(
            leaving.at[k, j], arriving.at[k, j], far_send.at[k, j], far_recv.at[k, j],
            "pair", target(j) * 2 + core,
        )

    for k in range(1, shards):
        arrival(k).start()
    moved[0] = mine[...]

    def product(j, to_core, right):
        left = blocks[target(j), to_core]
        return lax.dot_general(left, right, (((1,), (1,)), ((), ())), preferred_element_type=F32)

    def chunk(k, carry):
        @pl.when(k > 0)
        def _():
            arrival(k).wait_recv()

        def for_partner(j, carry):
            near_out[k, j] = product(j, 1 - core, moved[k]).astype(near_out.dtype)
            swap(k, j).start()
            return carry

        lax.fori_loop(0, chips, for_partner, 0)

        def for_line(j, carry):
            term = product(j, core, moved[k])
            swap(k, j).wait_recv()
            leaving[k, j] = (term + near_in[k, j].astype(F32)).astype(leaving.dtype)
            hand_over(k, j).start()
            return carry

        lax.fori_loop(0, last, for_line, 0)
        term = product(last, core, moved[k])
        swap(k, last).wait_recv()
        kept[k] = term + near_in[k, last].astype(F32)
        return carry

    lax.fori_loop(0, shards, chunk, 0)

    def collect(k, carry):
        total = kept[k]
        for j in range(last):
            hand_over(k, j).wait_recv()
            total = total + arriving[k, j].astype(F32)
        width = total.shape[1] // TAUS
        for t in range(TAUS):
            column = (t * shards + flipped(shard, k, shards)) * width
            out[:, pl.ds(pl.multiple_of(column, width), width)] = total[:, t * width:(t + 1) * width]
        for j in range(last):
            hand_over(k, j).wait_send()
        for j in range(chips):
            swap(k, j).wait_send()

        @pl.when(k > 0)
        def _():
            arrival(k).wait_send()

        return carry

    lax.fori_loop(0, shards, collect, 0)


def couple(blocks, moved, groups, shards):
    chips = groups // 2
    rows, depth = blocks.shape
    block = (rows // groups, moved.shape[0])
    return pl.pallas_call(
        functools.partial(coupling_kernel, chips, shards),
        out_shape=jax.ShapeDtypeStruct((block[0], shards * block[1]), F32),
        in_specs=[VMEM, VMEM],
        out_specs=VMEM,
        scratch_shapes=[
            pltpu.VMEM((shards,) + block, F32),
            pltpu.VMEM((shards,) + moved.shape, BF16),
            pltpu.VMEM((shards, chips) + block, BF16),
            pltpu.VMEM((shards, chips) + block, BF16),
            pltpu.VMEM((shards, chips - 1) + block, BF16),
            pltpu.VMEM((shards, chips - 1) + block, BF16),
        ]
        + [DMA((shards,))] * 2
        + [DMA((shards, chips))] * 2
        + [DMA((shards, chips - 1))] * 2,
        compiler_params=params(3),
    )(blocks.reshape(chips, 2, block[0], depth), moved)


def owned_rows(coefficient, names, group):
    local_blocks = coefficient.shape[0] // BS
    blocks = coefficient.reshape(local_blocks, BS, coefficient.shape[1])
    local_names = names - group * local_blocks
    owned = (local_names >= 0) & (local_names < local_blocks)
    picked = jnp.take(blocks, jnp.clip(local_names, 0, local_blocks - 1), axis=0)
    picked = jnp.where(owned[:, None, None], picked, jnp.zeros((), BF16))
    return picked.reshape(names.shape[0] * BS, coefficient.shape[1])


def own_gram(rows, energy, exponent_sign, tau_points, picks):
    factor = jnp.exp(exponent_sign * tau_points[:, None] * energy[None, :] / 2.0)
    scaled = (rows[None].astype(F32) * factor[:, None, :]).astype(BF16)
    own = jnp.concatenate(
        [lax.dynamic_slice_in_dim(scaled, pick * BS, BS, 1) for pick in picks], axis=1
    )
    return jnp.einsum("tin,tjn->tij", own, scaled, preferred_element_type=F32)


def per_device(groups, shards, c_occ, c_vir, e_occ, e_vir, tau_points, pair_blocks, block_count,
               three_center):
    own_slots = pair_blocks.shape[0]
    slot_total = own_slots * groups
    live_total = 5 * groups // 2
    group = lax.axis_index("pair")
    fields = 2 * own_slots + 1
    flat = jnp.concatenate([pair_blocks.reshape(-1), block_count])
    table = jnp.zeros((8, 128), jnp.int32).at[0, :fields].set(flat)
    tables = gather_table(table, groups)[:, 0, :fields]
    names = tables[:, :-1].reshape(slot_total, 2)
    counts = tables[:, -1]
    live = (jnp.arange(own_slots)[None, :] < counts[:, None]).reshape(slot_total)
    ids = jnp.arange(slot_total)
    ranks = jnp.sum(jnp.where(live[None, :] & (ids[None, :] < ids[:, None]), 1, 0), axis=1)
    select = live[None, :] & (ranks[None, :] == jnp.arange(live_total)[:, None])
    live_names = jnp.sum(jnp.where(select[:, :, None], names[None], 0), axis=1)
    rows = jnp.concatenate(
        [owned_rows(c_occ, live_names[:, 0], group), owned_rows(c_vir, live_names[:, 1], group)], axis=1
    )
    flat_blocks = three_center.reshape(three_center.shape[0], own_slots * BS * BS)
    rows, window = sum_rows(rows, flat_blocks[:WIN_DEV], groups)
    before = jnp.sum(jnp.where(jnp.arange(groups) < group, counts, 0))
    picks = [jnp.minimum(before + k, live_total - 1) for k in range(own_slots)]
    n_occ = c_occ.shape[1]
    terms = jnp.concatenate(
        [
            own_gram(rows[:, :n_occ], e_occ, 1.0, tau_points, picks),
            own_gram(rows[:, n_occ:], e_vir, -1.0, tau_points, picks),
        ],
        axis=0,
    )
    tiles = sum_tiles(terms.reshape(2 * TAUS * own_slots * BS, live_total * BS), shards)
    spread = (
        select[:, None, :, None] & jnp.eye(BS, dtype=bool)[None, :, None, :]
    ).astype(BF16).reshape(live_total * BS, slot_total * BS)
    tiles = jnp.dot(tiles, spread, preferred_element_type=F32).astype(BF16)
    tiles = tiles.reshape(2, TAUS, own_slots, BS, slot_total, BS)
    occ_tiles, vir_tiles = tiles[0], tiles[1]
    blocks = window.reshape(groups, WIN_DEV, own_slots, BS, BS).transpose(1, 0, 2, 3, 4)
    blocks = blocks.reshape(WIN_DEV, slot_total, BS, BS)
    half_moved = jnp.einsum(
        "tkisj,psjl->tpksil", occ_tiles, blocks, preferred_element_type=F32
    ).astype(BF16)
    moved = jnp.einsum("tpksil,tkmsl->tpkim", half_moved, vir_tiles, preferred_element_type=F32)
    live_mask = jnp.arange(own_slots) < block_count[0]
    moved = moved * live_mask.astype(F32)[None, None, :, None, None]
    transformed = moved.astype(BF16).reshape(TAUS * WIN_DEV, own_slots * BS * BS)
    coupling = couple(flat_blocks, transformed, groups, shards)
    return coupling.reshape(coupling.shape[0], TAUS, shards * WIN_DEV)


def solution(mesh):
    placed = (
        P("pair", "aux"),
        P("pair", "aux"),
        P("aux"),
        P("aux"),
        P(),
        P("pair", None),
        P("pair"),
        P("aux", "pair", None),
    )
    return jax.shard_map(
        functools.partial(per_device, mesh.shape["pair"], mesh.shape["aux"]),
        mesh=mesh,
        in_specs=placed,
        out_specs=P(("aux", "pair"), None, None),
        check_vma=False,
    )
```

```python
import functools

import jax
import jax.numpy as jnp
from jax import lax
from jax.experimental import pallas as pl
from jax.experimental.pallas import tpu as pltpu
from jax.sharding import PartitionSpec as P

BS = 16
TAUS = 2
WIN_DEV = 128
PAIRS = 2
HOP = 2
MESH = pl.DeviceIdType.MESH
VMEM = pl.BlockSpec(memory_space=pltpu.VMEM)
DMA = pltpu.SemaphoreType.DMA
BF16 = jnp.bfloat16
F32 = jnp.float32


def params(collective_id):
    return pltpu.CompilerParams(
        collective_id=collective_id, has_side_effects=True, vmem_limit_bytes=40 * 2**20
    )


def greet(pair_peers, aux_peers=()):
    barrier = pltpu.get_barrier_semaphore()
    for peer in pair_peers:
        pl.semaphore_signal(barrier, inc=1, device_id={"pair": peer}, device_id_type=MESH)
    for peer in aux_peers:
        pl.semaphore_signal(barrier, inc=1, device_id={"aux": peer}, device_id_type=MESH)
    pl.semaphore_wait(barrier, len(pair_peers) + len(aux_peers))


def remote(source, target, send, received, axis, device):
    return pltpu.make_async_remote_copy(
        src_ref=source,
        dst_ref=target,
        send_sem=send,
        recv_sem=received,
        device_id={axis: device},
        device_id_type=MESH,
    )


def place():
    me = lax.axis_index("pair")
    core = lax.rem(me, 2)
    return me, core, me // 2, me + 1 - 2 * core


def table_kernel(groups, mine, out, send, received):
    me = lax.axis_index("pair")
    peers = [lax.rem(me + k, groups) for k in range(1, groups)]
    greet(peers)
    copies = []
    for k in range(groups - 1):
        copy = remote(mine, out.at[me], send.at[k], received.at[k], "pair", peers[k])
        copy.start()
        copies.append(copy)
    out[me] = mine[...]
    for copy in copies:
        copy.wait()


def gather_table(table, groups):
    return pl.pallas_call(
        functools.partial(table_kernel, groups),
        out_shape=jax.ShapeDtypeStruct((groups,) + table.shape, table.dtype),
        in_specs=[VMEM],
        out_specs=VMEM,
        scratch_shapes=[DMA((groups - 1,)), DMA((groups - 1,))],
        compiler_params=params(0),
    )(table)


def rows_kernel(chips, chunks, rows, window, out, blocks,
                own, right_in, left_in, right_out, left_out,
                own_send, own_recv, right_send, right_recv, left_send, left_recv,
                done_send, done_recv, far_send, far_recv, near_send, near_recv):
    me, core, chip, partner = place()
    last = chips - 1
    after = lax.rem(me + 2, 2 * chips)
    before = lax.rem(me + 2 * chips - 2, 2 * chips)
    line = [lax.rem(chip + k, chips) * 2 + core for k in range(1, chips)]
    greet([partner] + line)

    def swap(j):
        return remote(rows.at[1 - core, j], own.at[j], own_send.at[j], own_recv.at[j], "pair", partner)

    def rightward(j):
        return remote(right_out.at[j], right_in.at[j], right_send.at[j], right_recv.at[j], "pair", after)

    def leftward(j):
        return remote(left_out.at[j], left_in.at[j], left_send.at[j], left_recv.at[j], "pair", before)

    def finished(j):
        return remote(out.at[core, j], out.at[core, j], done_send.at[j], done_recv.at[j], "pair", partner)

    def start_swap(j, carry):
        swap(j).start()
        return carry

    lax.fori_loop(0, chunks, start_swap, 0)
    far = []
    for k, peer in enumerate(line):
        far.append(remote(window, blocks.at[me], far_send.at[k], far_recv.at[k], "pair", peer))
    near = [remote(window, blocks.at[me], near_send.at[0], near_recv.at[0], "pair", partner)]
    near[0].start()
    blocks[me] = window[...]

    def step(i, carry):
        @pl.when(i < chunks)
        def _():
            swap(i).wait_recv()
            own[i] = own[i] + rows[core, i]

        to_right = i - HOP * chip

        @pl.when((to_right >= 0) & (to_right < chunks))
        def _():
            @pl.when(chip > 0)
            def _():
                rightward(to_right).wait_recv()

            @pl.when(chip == 0)
            def _():
                right_out[to_right] = own[to_right]

            @pl.when((chip > 0) & (chip < last))
            def _():
                right_out[to_right] = own[to_right] + right_in[to_right]

            @pl.when(chip < last)
            def _():
                rightward(to_right).start()

        to_left = i - HOP * (last - chip)

        @pl.when((to_left >= 0) & (to_left < chunks))
        def _():
            @pl.when(chip < last)
            def _():
                leftward(to_left).wait_recv()

            @pl.when(chip == last)
            def _():
                left_out[to_left] = own[to_left]

            @pl.when((chip > 0) & (chip < last))
            def _():
                left_out[to_left] = own[to_left] + left_in[to_left]

            @pl.when(chip > 0)
            def _():
                leftward(to_left).start()

        ready = i - HOP * jnp.maximum(chip, last - chip)

        @pl.when((ready >= 0) & (ready < chunks))
        def _():
            @pl.when(chip == 0)
            def _():
                out[core, ready] = own[ready] + left_in[ready]

            @pl.when(chip == last)
            def _():
                out[core, ready] = own[ready] + right_in[ready]

            @pl.when((chip > 0) & (chip < last))
            def _():
                out[core, ready] = own[ready] + left_in[ready] + right_in[ready]

            finished(ready).start()

        return carry

    lax.fori_loop(0, HOP * last, step, 0)
    for copy in far:
        copy.start()
    lax.fori_loop(HOP * last, chunks + HOP * last, step, 0)
    for k, copy in enumerate(far):
        copy.wait_recv()
        origin = lax.rem(chip + last - k, chips) * 2 + core
        pass_on = remote(
            blocks.at[origin], blocks.at[origin], near_send.at[k + 1], near_recv.at[k + 1], "pair", partner
        )
        pass_on.start()
        near.append(pass_on)

    def drain(j, carry):
        swap(j).wait_send()

        @pl.when(chip < last)
        def _():
            rightward(j).wait_send()

        @pl.when(chip > 0)
        def _():
            leftward(j).wait_send()

        finished(j).wait_send()
        remote(
            out.at[1 - core, j], out.at[1 - core, j], done_send.at[j], done_recv.at[j], "pair", partner
        ).wait_recv()
        return carry

    lax.fori_loop(0, chunks, drain, 0)
    for copy in near:
        copy.wait()
    for copy in far:
        copy.wait_send()


def sum_rows(rows, window, groups):
    chunks = rows.shape[0] // (2 * BS)
    width = rows.shape[1]
    shape = (2, chunks, BS, width)
    chips = groups // 2
    summed, blocks = pl.pallas_call(
        functools.partial(rows_kernel, chips, chunks),
        out_shape=(
            jax.ShapeDtypeStruct(shape, rows.dtype),
            jax.ShapeDtypeStruct((groups,) + window.shape, window.dtype),
        ),
        in_specs=[VMEM, VMEM],
        out_specs=(VMEM, VMEM),
        scratch_shapes=[pltpu.VMEM(shape[1:], rows.dtype)] * 5
        + [DMA((chunks,))] * 8
        + [DMA((chips - 1,))] * 2
        + [DMA((chips,))] * 2,
        compiler_params=params(1),
    )(rows.reshape(shape), window)
    return summed.reshape(rows.shape), blocks


def tiles_kernel(shards, terms, tiles, held, term_send, term_recv, tile_send, tile_recv):
    shard = lax.axis_index("aux")
    peers = [flipped(shard, k, shards) for k in range(1, shards)]
    greet([], peers)
    parts = []
    for k, peer in enumerate(peers):
        copy = remote(terms.at[peer], held.at[k], term_send.at[k], term_recv.at[k], "aux", peer)
        copy.start()
        parts.append(copy)
    total = terms[shard]
    for k, copy in enumerate(parts):
        copy.wait_recv()
        total = total + held[k]
    tiles[shard] = total.astype(tiles.dtype)
    sums = []
    for k, peer in enumerate(peers):
        copy = remote(tiles.at[shard], tiles.at[shard], tile_send.at[k], tile_recv.at[k], "aux", peer)
        copy.start()
        sums.append(copy)
    for copy in sums:
        copy.wait()
    for copy in parts:
        copy.wait_send()


def sum_tiles(terms, shards):
    rows, width = terms.shape
    grouped = (shards, rows // shards, width)
    tiles = pl.pallas_call(
        functools.partial(tiles_kernel, shards),
        out_shape=jax.ShapeDtypeStruct(grouped, BF16),
        in_specs=[VMEM],
        out_specs=VMEM,
        scratch_shapes=[pltpu.VMEM((shards - 1,) + grouped[1:], F32)] + [DMA((shards - 1,))] * 4,
        compiler_params=params(2),
    )(terms.reshape(grouped))
    return tiles.reshape(rows, width)


def flipped(shard, k, shards):
    other, bit = 0, 1
    while bit < shards:
        other = other + lax.rem(shard // bit + k // bit, 2) * bit
        bit = bit * 2
    return other


def coupling_kernel(chips, shards, blocks, mine, out, kept, moved, near_out, near_in, leaving, arriving,
                    moved_send, moved_recv, near_send, near_recv, far_send, far_recv):
    me, core, chip, partner = place()
    shard = lax.axis_index("aux")
    last = chips - 1
    peers = [flipped(shard, k, shards) for k in range(1, shards)]
    greet([partner] + [lax.rem(chip + k, chips) * 2 + core for k in range(1, chips)], peers)

    def arrival(k):
        return remote(
            mine, moved.at[k], moved_send.at[k], moved_recv.at[k], "aux", flipped(shard, k, shards)
        )

    def target(j):
        return lax.rem(chip + 1 + j, chips)

    def swap(k, j):
        return remote(
            near_out.at[k, j], near_in.at[k, j], near_send.at[k, j], near_recv.at[k, j], "pair", partner
        )

    def hand_over(k, j):
        return remote(
            leaving.at[k, j], arriving.at[k, j], far_send.at[k, j], far_recv.at[k, j],
            "pair", target(j) * 2 + core,
        )

    for k in range(1, shards):
        arrival(k).start()
    moved[0] = mine[...]

    def product(j, to_core, right):
        left = blocks[target(j), to_core]
        return lax.dot_general(left, right, (((1,), (1,)), ((), ())), preferred_element_type=F32)

    def chunk(k, carry):
        @pl.when(k > 0)
        def _():
            arrival(k).wait_recv()

        def for_partner(j, carry):
            near_out[k, j] = product(j, 1 - core, moved[k]).astype(near_out.dtype)
            swap(k, j).start()
            return carry

        lax.fori_loop(0, chips, for_partner, 0)

        def for_line(j, carry):
            term = product(j, core, moved[k])
            swap(k, j).wait_recv()
            leaving[k, j] = (term + near_in[k, j].astype(F32)).astype(leaving.dtype)
            hand_over(k, j).start()
            return carry

        lax.fori_loop(0, last, for_line, 0)
        term = product(last, core, moved[k])
        swap(k, last).wait_recv()
        kept[k] = term + near_in[k, last].astype(F32)
        return carry

    lax.fori_loop(0, shards, chunk, 0)

    def collect(k, carry):
        total = kept[k]
        for j in range(last):
            hand_over(k, j).wait_recv()
            total = total + arriving[k, j].astype(F32)
        width = total.shape[1] // TAUS
        for t in range(TAUS):
            column = (t * shards + flipped(shard, k, shards)) * width
            out[:, pl.ds(pl.multiple_of(column, width), width)] = total[:, t * width:(t + 1) * width]
        for j in range(last):
            hand_over(k, j).wait_send()
        for j in range(chips):
            swap(k, j).wait_send()

        @pl.when(k > 0)
        def _():
            arrival(k).wait_send()

        return carry

    lax.fori_loop(0, shards, collect, 0)


def couple(blocks, moved, groups, shards):
    chips = groups // 2
    rows, depth = blocks.shape
    block = (rows // groups, moved.shape[0])
    return pl.pallas_call(
        functools.partial(coupling_kernel, chips, shards),
        out_shape=jax.ShapeDtypeStruct((block[0], shards * block[1]), F32),
        in_specs=[VMEM, VMEM],
        out_specs=VMEM,
        scratch_shapes=[
            pltpu.VMEM((shards,) + block, F32),
            pltpu.VMEM((shards,) + moved.shape, BF16),
            pltpu.VMEM((shards, chips) + block, BF16),
            pltpu.VMEM((shards, chips) + block, BF16),
            pltpu.VMEM((shards, chips - 1) + block, BF16),
            pltpu.VMEM((shards, chips - 1) + block, BF16),
        ]
        + [DMA((shards,))] * 2
        + [DMA((shards, chips))] * 2
        + [DMA((shards, chips - 1))] * 2,
        compiler_params=params(3),
    )(blocks.reshape(chips, 2, block[0], depth), moved)


def moved_kernel(own_slots, slots_ref, occ, vir, blocks, out, half):
    live_total, size, width = occ.shape
    fold_rows = blocks.shape[2]
    pairs = fold_rows // (own_slots * size)
    wide = pairs * width
    rank = lax.broadcasted_iota(jnp.int32, (pairs * own_slots, size, wide), 0)
    side = lax.broadcasted_iota(jnp.int32, (pairs * own_slots, size, wide), 2) // width

    def one_slot(n, carry):
        slot = slots_ref[n]
        tile = occ[n].astype(F32)
        spread = jnp.concatenate([tile] * pairs, axis=1)[None]
        spread = jnp.where(rank == side * own_slots + lax.rem(slot, own_slots), spread, 0.0)
        spread = spread.reshape(fold_rows, wide).astype(BF16)
        half[n] = jnp.dot(
            blocks[slot // own_slots], spread, preferred_element_type=F32
        ).astype(BF16)
        return carry

    lax.fori_loop(0, live_total, one_slot, 0)
    row = lax.broadcasted_iota(jnp.int32, (width, wide), 0) // size
    column = lax.rem(lax.broadcasted_iota(jnp.int32, (width, wide), 1), width) // size
    same = row == column
    entry = lax.broadcasted_iota(jnp.int32, (pairs * size, wide), 0)
    lane = lax.broadcasted_iota(jnp.int32, (pairs * size, wide), 1)
    fold = jnp.where(entry == lane // width * size + lax.rem(lane, size), 1.0, 0.0).astype(BF16)

    def one_pair(at, carry):
        rows = pl.ds(pl.multiple_of(at * size, size), size)
        right = half[:, rows, :].reshape(live_total * size, wide)
        summed = jnp.dot(vir[...], right, preferred_element_type=F32)
        summed = jnp.where(same, summed, 0.0).astype(BF16)
        out[at] = lax.dot_general(
            fold, summed, (((1,), (1,)), ((), ())), preferred_element_type=F32
        ).astype(BF16)
        return carry

    lax.fori_loop(0, out.shape[0], one_pair, 0, unroll=4)


def move(slots, occ, vir, blocks, own_slots):
    live_total, size, width = occ.shape
    wide = blocks.shape[2] // (own_slots * size) * width
    rows = blocks.shape[1]
    return pl.pallas_call(
        functools.partial(moved_kernel, own_slots),
        out_shape=jax.ShapeDtypeStruct((rows // size, wide // width * size, width), BF16),
        in_specs=[pl.BlockSpec(memory_space=pltpu.SMEM), VMEM, VMEM, VMEM],
        out_specs=VMEM,
        scratch_shapes=[pltpu.VMEM((live_total, rows, wide), BF16)],
        compiler_params=pltpu.CompilerParams(vmem_limit_bytes=40 * 2**20),
    )(slots, occ, vir, blocks)


def owned_rows(coefficient, names, group):
    local_blocks = coefficient.shape[0] // BS
    blocks = coefficient.reshape(local_blocks, BS, coefficient.shape[1])
    local_names = names - group * local_blocks
    owned = (local_names >= 0) & (local_names < local_blocks)
    picked = jnp.take(blocks, jnp.clip(local_names, 0, local_blocks - 1), axis=0)
    picked = jnp.where(owned[:, None, None], picked, jnp.zeros((), BF16))
    return picked.reshape(names.shape[0] * BS, coefficient.shape[1])


def own_gram(rows, energy, exponent_sign, tau_points, picks):
    factor = jnp.exp(exponent_sign * tau_points[:, None] * energy[None, :] / 2.0)
    scaled = (rows[None].astype(F32) * factor[:, None, :]).astype(BF16)
    own = jnp.concatenate(
        [lax.dynamic_slice_in_dim(scaled, pick * BS, BS, 1) for pick in picks], axis=1
    )
    return jnp.einsum("tin,tjn->tij", own, scaled, preferred_element_type=F32)


def per_device(groups, shards, c_occ, c_vir, e_occ, e_vir, tau_points, pair_blocks, block_count,
               three_center):
    own_slots = pair_blocks.shape[0]
    slot_total = own_slots * groups
    live_total = 5 * groups // 2
    group = lax.axis_index("pair")
    fields = 2 * own_slots + 1
    flat = jnp.concatenate([pair_blocks.reshape(-1), block_count])
    table = jnp.zeros((8, 128), jnp.int32).at[0, :fields].set(flat)
    tables = gather_table(table, groups)[:, 0, :fields]
    names = tables[:, :-1].reshape(slot_total, 2)
    counts = tables[:, -1]
    live = (jnp.arange(own_slots)[None, :] < counts[:, None]).reshape(slot_total)
    ids = jnp.arange(slot_total)
    ranks = jnp.sum(jnp.where(live[None, :] & (ids[None, :] < ids[:, None]), 1, 0), axis=1)
    select = live[None, :] & (ranks[None, :] == jnp.arange(live_total)[:, None])
    live_names = jnp.sum(jnp.where(select[:, :, None], names[None], 0), axis=1)
    rows = jnp.concatenate(
        [owned_rows(c_occ, live_names[:, 0], group), owned_rows(c_vir, live_names[:, 1], group)], axis=1
    )
    flat_blocks = three_center.reshape(three_center.shape[0], own_slots * BS * BS)
    window = three_center[:WIN_DEV].reshape(PAIRS, WIN_DEV // PAIRS, own_slots, BS, BS)
    window = window.transpose(1, 4, 0, 2, 3).reshape(WIN_DEV // PAIRS * BS, PAIRS * own_slots * BS)
    rows, blocks = sum_rows(rows, window, groups)
    before = jnp.sum(jnp.where(jnp.arange(groups) < group, counts, 0))
    picks = [jnp.minimum(before + k, live_total - 1) for k in range(own_slots)]
    n_occ = c_occ.shape[1]
    terms = jnp.concatenate(
        [
            own_gram(rows[:, :n_occ], e_occ, 1.0, tau_points, picks),
            own_gram(rows[:, n_occ:], e_vir, -1.0, tau_points, picks),
        ],
        axis=0,
    )
    tiles = sum_tiles(terms.reshape(2 * TAUS * own_slots * BS, live_total * BS), shards)
    width = TAUS * own_slots * BS
    live_ids = jnp.sum(jnp.where(select, ids[None, :], 0), axis=1)
    occ_tiles = tiles[:width].T.reshape(live_total, BS, width)
    moved = move(live_ids, occ_tiles, tiles[width:], blocks, own_slots)
    moved = moved.reshape(WIN_DEV // PAIRS, PAIRS, BS, TAUS, own_slots, BS)
    live_mask = jnp.arange(own_slots) < block_count[0]
    moved = jnp.where(live_mask[:, None], moved, jnp.zeros((), BF16))
    transformed = moved.transpose(3, 1, 0, 4, 2, 5).reshape(TAUS * WIN_DEV, own_slots * BS * BS)
    coupling = couple(flat_blocks, transformed, groups, shards)
    return coupling.reshape(coupling.shape[0], TAUS, shards * WIN_DEV)


def solution(mesh):
    placed = (
        P("pair", "aux"),
        P("pair", "aux"),
        P("aux"),
        P("aux"),
        P(),
        P("pair", None),
        P("pair"),
        P("aux", "pair", None),
    )
    return jax.shard_map(
        functools.partial(per_device, mesh.shape["pair"], mesh.shape["aux"]),
        mesh=mesh,
        in_specs=placed,
        out_specs=P(("aux", "pair"), None, None),
        check_vma=False,
    )
```

```python
import functools

import jax
import jax.numpy as jnp
from jax import lax
from jax.experimental import pallas as pl
from jax.experimental.pallas import tpu as pltpu
from jax.sharding import PartitionSpec as P

BS = 16
TAUS = 2
WIN_DEV = 128
PAIRS = 2
HOP = 2
MESH = pl.DeviceIdType.MESH
VMEM = pl.BlockSpec(memory_space=pltpu.VMEM)
DMA = pltpu.SemaphoreType.DMA
BF16 = jnp.bfloat16
F32 = jnp.float32


def params(collective_id):
    return pltpu.CompilerParams(
        collective_id=collective_id, has_side_effects=True, vmem_limit_bytes=40 * 2**20
    )


def greet(pair_peers, aux_peers=()):
    barrier = pltpu.get_barrier_semaphore()
    for peer in pair_peers:
        pl.semaphore_signal(barrier, inc=1, device_id={"pair": peer}, device_id_type=MESH)
    for peer in aux_peers:
        pl.semaphore_signal(barrier, inc=1, device_id={"aux": peer}, device_id_type=MESH)
    pl.semaphore_wait(barrier, len(pair_peers) + len(aux_peers))


def remote(source, target, send, received, axis, device):
    return pltpu.make_async_remote_copy(
        src_ref=source,
        dst_ref=target,
        send_sem=send,
        recv_sem=received,
        device_id={axis: device},
        device_id_type=MESH,
    )


def place():
    me = lax.axis_index("pair")
    core = lax.rem(me, 2)
    return me, core, me // 2, me + 1 - 2 * core


def table_kernel(groups, mine, out, send, received):
    me = lax.axis_index("pair")
    peers = [lax.rem(me + k, groups) for k in range(1, groups)]
    greet(peers)
    copies = []
    for k in range(groups - 1):
        copy = remote(mine, out.at[me], send.at[k], received.at[k], "pair", peers[k])
        copy.start()
        copies.append(copy)
    out[me] = mine[...]
    for copy in copies:
        copy.wait()


def gather_table(table, groups):
    return pl.pallas_call(
        functools.partial(table_kernel, groups),
        out_shape=jax.ShapeDtypeStruct((groups,) + table.shape, table.dtype),
        in_specs=[VMEM],
        out_specs=VMEM,
        scratch_shapes=[DMA((groups - 1,)), DMA((groups - 1,))],
        compiler_params=params(0),
    )(table)


def rows_kernel(chips, chunks, pieces, rows, window, whole, out, blocks, flat,
                own, right_in, left_in, right_out, left_out,
                own_send, own_recv, right_send, right_recv, left_send, left_recv,
                done_send, done_recv, far_send, far_recv, near_send, near_recv):
    me, core, chip, partner = place()
    last = chips - 1
    after = lax.rem(me + 2, 2 * chips)
    before = lax.rem(me + 2 * chips - 2, 2 * chips)
    line = [lax.rem(chip + k, chips) * 2 + core for k in range(1, chips)]
    greet([partner] + line)

    def swap(j):
        return remote(rows.at[1 - core, j], own.at[j], own_send.at[j], own_recv.at[j], "pair", partner)

    def rightward(j):
        return remote(right_out.at[j], right_in.at[j], right_send.at[j], right_recv.at[j], "pair", after)

    def leftward(j):
        return remote(left_out.at[j], left_in.at[j], left_send.at[j], left_recv.at[j], "pair", before)

    def finished(j):
        return remote(out.at[core, j], out.at[core, j], done_send.at[j], done_recv.at[j], "pair", partner)

    def start_swap(j, carry):
        swap(j).start()
        return carry

    lax.fori_loop(0, chunks, start_swap, 0)
    far = []
    for k, peer in enumerate(line):
        far.append(remote(window, blocks.at[me], far_send.at[k], far_recv.at[k], "pair", peer))
    near = [remote(window, blocks.at[me], near_send.at[0], near_recv.at[0], "pair", partner)]
    near[0].start()
    blocks[me] = window[...]

    def step(i, carry):
        @pl.when(i < pieces)
        def _():
            count, depth = whole.shape[0] // pieces, whole.shape[2]
            at = pl.ds(pl.multiple_of(i * count, BS), count)
            part = whole[at].astype(F32)
            for k in range(whole.shape[1]):
                flat[at, k * depth:(k + 1) * depth] = part[:, k, :].astype(flat.dtype)

        @pl.when(i < chunks)
        def _():
            swap(i).wait_recv()
            own[i] = own[i] + rows[core, i]

        to_right = i - HOP * chip

        @pl.when((to_right >= 0) & (to_right < chunks))
        def _():
            @pl.when(chip > 0)
            def _():
                rightward(to_right).wait_recv()

            @pl.when(chip == 0)
            def _():
                right_out[to_right] = own[to_right]

            @pl.when((chip > 0) & (chip < last))
            def _():
                right_out[to_right] = own[to_right] + right_in[to_right]

            @pl.when(chip < last)
            def _():
                rightward(to_right).start()

        to_left = i - HOP * (last - chip)

        @pl.when((to_left >= 0) & (to_left < chunks))
        def _():
            @pl.when(chip < last)
            def _():
                leftward(to_left).wait_recv()

            @pl.when(chip == last)
            def _():
                left_out[to_left] = own[to_left]

            @pl.when((chip > 0) & (chip < last))
            def _():
                left_out[to_left] = own[to_left] + left_in[to_left]

            @pl.when(chip > 0)
            def _():
                leftward(to_left).start()

        ready = i - HOP * jnp.maximum(chip, last - chip)

        @pl.when((ready >= 0) & (ready < chunks))
        def _():
            @pl.when(chip == 0)
            def _():
                out[core, ready] = own[ready] + left_in[ready]

            @pl.when(chip == last)
            def _():
                out[core, ready] = own[ready] + right_in[ready]

            @pl.when((chip > 0) & (chip < last))
            def _():
                out[core, ready] = own[ready] + left_in[ready] + right_in[ready]

            finished(ready).start()

        return carry

    lax.fori_loop(0, HOP * last, step, 0)
    for copy in far:
        copy.start()
    lax.fori_loop(HOP * last, chunks + HOP * last, step, 0)
    for k, copy in enumerate(far):
        copy.wait_recv()
        origin = lax.rem(chip + last - k, chips) * 2 + core
        pass_on = remote(
            blocks.at[origin], blocks.at[origin], near_send.at[k + 1], near_recv.at[k + 1], "pair", partner
        )
        pass_on.start()
        near.append(pass_on)

    def drain(j, carry):
        swap(j).wait_send()

        @pl.when(chip < last)
        def _():
            rightward(j).wait_send()

        @pl.when(chip > 0)
        def _():
            leftward(j).wait_send()

        finished(j).wait_send()
        remote(
            out.at[1 - core, j], out.at[1 - core, j], done_send.at[j], done_recv.at[j], "pair", partner
        ).wait_recv()
        return carry

    lax.fori_loop(0, chunks, drain, 0)
    for copy in near:
        copy.wait()
    for copy in far:
        copy.wait_send()


def sum_rows(rows, window, whole, groups):
    chunks = rows.shape[0] // (2 * BS)
    width = rows.shape[1]
    shape = (2, chunks, BS, width)
    chips = groups // 2
    units = whole.shape[0] // BS
    steps = chunks + HOP * (chips - 1)
    pieces = max(d for d in range(1, steps + 1) if units % d == 0)
    flat_shape = (whole.shape[0], whole.shape[1] * whole.shape[2])
    summed, blocks, flat = pl.pallas_call(
        functools.partial(rows_kernel, chips, chunks, pieces),
        out_shape=(
            jax.ShapeDtypeStruct(shape, rows.dtype),
            jax.ShapeDtypeStruct((groups,) + window.shape, window.dtype),
            jax.ShapeDtypeStruct(flat_shape, whole.dtype),
        ),
        in_specs=[VMEM, VMEM, VMEM],
        out_specs=(VMEM, VMEM, VMEM),
        scratch_shapes=[pltpu.VMEM(shape[1:], rows.dtype)] * 5
        + [DMA((chunks,))] * 8
        + [DMA((chips - 1,))] * 2
        + [DMA((chips,))] * 2,
        compiler_params=params(1),
    )(rows.reshape(shape), window, whole)
    return summed.reshape(rows.shape), blocks, flat


def tiles_kernel(shards, terms, tiles, held, term_send, term_recv, tile_send, tile_recv):
    shard = lax.axis_index("aux")
    peers = [flipped(shard, k, shards) for k in range(1, shards)]
    greet([], peers)
    parts = []
    for k, peer in enumerate(peers):
        copy = remote(terms.at[peer], held.at[k], term_send.at[k], term_recv.at[k], "aux", peer)
        copy.start()
        parts.append(copy)
    total = terms[shard]
    for k, copy in enumerate(parts):
        copy.wait_recv()
        total = total + held[k]
    tiles[shard] = total.astype(tiles.dtype)
    sums = []
    for k, peer in enumerate(peers):
        copy = remote(tiles.at[shard], tiles.at[shard], tile_send.at[k], tile_recv.at[k], "aux", peer)
        copy.start()
        sums.append(copy)
    for copy in sums:
        copy.wait()
    for copy in parts:
        copy.wait_send()


def sum_tiles(terms, shards):
    rows, width = terms.shape
    grouped = (shards, rows // shards, width)
    tiles = pl.pallas_call(
        functools.partial(tiles_kernel, shards),
        out_shape=jax.ShapeDtypeStruct(grouped, BF16),
        in_specs=[VMEM],
        out_specs=VMEM,
        scratch_shapes=[pltpu.VMEM((shards - 1,) + grouped[1:], F32)] + [DMA((shards - 1,))] * 4,
        compiler_params=params(2),
    )(terms.reshape(grouped))
    return tiles.reshape(rows, width)


def flipped(shard, k, shards):
    other, bit = 0, 1
    while bit < shards:
        other = other + lax.rem(shard // bit + k // bit, 2) * bit
        bit = bit * 2
    return other


def coupling_kernel(chips, shards, blocks, mine, out, kept, moved, total, near_out, near_in,
                    right_out, right_in, left_out, left_in, moved_send, moved_recv,
                    near_send, near_recv, right_send, right_recv, left_send, left_recv):
    me, core, chip, partner = place()
    shard = lax.axis_index("aux")
    last = chips - 1
    after = lax.rem(me + 2, 2 * chips)
    before = lax.rem(me + 2 * chips - 2, 2 * chips)
    peers = [flipped(shard, k, shards) for k in range(1, shards)]
    greet([partner, after, before], peers)

    def arrival(k):
        return remote(
            mine, moved.at[k], moved_send.at[k], moved_recv.at[k], "aux", flipped(shard, k, shards)
        )

    def swap(k, to):
        return remote(
            near_out.at[k, to], near_in.at[k, to], near_send.at[k, to], near_recv.at[k, to],
            "pair", partner,
        )

    def rightward(k, to):
        return remote(
            right_out.at[k, to], right_in.at[k, to], right_send.at[k, to], right_recv.at[k, to],
            "pair", after,
        )

    def leftward(k, to):
        return remote(
            left_out.at[k, to], left_in.at[k, to], left_send.at[k, to], left_recv.at[k, to],
            "pair", before,
        )

    for k in range(1, shards):
        arrival(k).start()
    moved[0] = mine[...]

    def product(to, to_core, right):
        return lax.dot_general(
            blocks[to, to_core], right, (((1,), (1,)), ((), ())), preferred_element_type=F32
        )

    def chip_sum(k, to):
        term = product(to, core, moved[k])
        swap(k, to).wait_recv()
        return term + near_in[k, to].astype(F32)

    def chunk(k, carry):
        @pl.when(k > 0)
        def _():
            arrival(k).wait_recv()

        def for_partner(j, carry):
            to = last - j
            near_out[k, to] = product(to, 1 - core, moved[k]).astype(near_out.dtype)
            swap(k, to).start()
            return carry

        lax.fori_loop(0, chips, for_partner, 0)

        def for_right(j, carry):
            to = last - j

            @pl.when(to > chip)
            def _():
                total[...] = chip_sum(k, to)

                @pl.when(chip > 0)
                def _():
                    rightward(k, to).wait_recv()
                    total[...] += right_in[k, to].astype(F32)

                right_out[k, to] = total[...].astype(right_out.dtype)
                rightward(k, to).start()

            return carry

        lax.fori_loop(0, last, for_right, 0)

        def for_left(to, carry):
            @pl.when(to < chip)
            def _():
                total[...] = chip_sum(k, to)

                @pl.when(chip < last)
                def _():
                    leftward(k, to).wait_recv()
                    total[...] += left_in[k, to].astype(F32)

                left_out[k, to] = total[...].astype(left_out.dtype)
                leftward(k, to).start()

            return carry

        lax.fori_loop(0, last, for_left, 0)
        kept[k] = chip_sum(k, chip)
        return carry

    lax.fori_loop(0, shards, chunk, 0)

    def collect(k, carry):
        @pl.when(chip > 0)
        def _():
            rightward(k, chip).wait_recv()
            kept[k] = kept[k] + right_in[k, chip].astype(F32)

        @pl.when(chip < last)
        def _():
            leftward(k, chip).wait_recv()
            kept[k] = kept[k] + left_in[k, chip].astype(F32)

        width = kept.shape[2] // TAUS
        for t in range(TAUS):
            column = (t * shards + flipped(shard, k, shards)) * width
            out[:, pl.ds(pl.multiple_of(column, width), width)] = kept[k, :, t * width:(t + 1) * width]

        def sent(to, carry):
            swap(k, to).wait_send()

            @pl.when(to > chip)
            def _():
                rightward(k, to).wait_send()

            @pl.when(to < chip)
            def _():
                leftward(k, to).wait_send()

            return carry

        lax.fori_loop(0, chips, sent, 0)

        @pl.when(k > 0)
        def _():
            arrival(k).wait_send()

        return carry

    lax.fori_loop(0, shards, collect, 0)


def couple(blocks, moved, groups, shards):
    chips = groups // 2
    rows, depth = blocks.shape
    block = (rows // groups, moved.shape[0])
    return pl.pallas_call(
        functools.partial(coupling_kernel, chips, shards),
        out_shape=jax.ShapeDtypeStruct((block[0], shards * block[1]), F32),
        in_specs=[VMEM, VMEM],
        out_specs=VMEM,
        scratch_shapes=[
            pltpu.VMEM((shards,) + block, F32),
            pltpu.VMEM((shards,) + moved.shape, BF16),
            pltpu.VMEM(block, F32),
        ]
        + [pltpu.VMEM((shards, chips) + block, BF16)] * 6
        + [DMA((shards,))] * 2
        + [DMA((shards, chips))] * 6,
        compiler_params=params(3),
    )(blocks.reshape(chips, 2, block[0], depth), moved)


def moved_kernel(own_slots, slots_ref, occ, vir, blocks, out, half):
    live_total, size, width = occ.shape
    fold_rows = blocks.shape[2]
    pairs = fold_rows // (own_slots * size)
    wide = pairs * width
    rank = lax.broadcasted_iota(jnp.int32, (pairs * own_slots, size, wide), 0)
    side = lax.broadcasted_iota(jnp.int32, (pairs * own_slots, size, wide), 2) // width

    def one_slot(n, carry):
        slot = slots_ref[n]
        tile = occ[n].astype(F32)
        spread = jnp.concatenate([tile] * pairs, axis=1)[None]
        spread = jnp.where(rank == side * own_slots + lax.rem(slot, own_slots), spread, 0.0)
        spread = spread.reshape(fold_rows, wide).astype(BF16)
        half[n] = jnp.dot(
            blocks[slot // own_slots], spread, preferred_element_type=F32
        ).astype(BF16)
        return carry

    lax.fori_loop(0, live_total, one_slot, 0)
    row = lax.broadcasted_iota(jnp.int32, (width, wide), 0) // size
    column = lax.rem(lax.broadcasted_iota(jnp.int32, (width, wide), 1), width) // size
    same = row == column
    entry = lax.broadcasted_iota(jnp.int32, (pairs * size, wide), 0)
    lane = lax.broadcasted_iota(jnp.int32, (pairs * size, wide), 1)
    fold = jnp.where(entry == lane // width * size + lax.rem(lane, size), 1.0, 0.0).astype(BF16)

    def one_pair(at, carry):
        rows = pl.ds(pl.multiple_of(at * size, size), size)
        right = half[:, rows, :].reshape(live_total * size, wide)
        summed = jnp.dot(vir[...], right, preferred_element_type=F32)
        summed = jnp.where(same, summed, 0.0).astype(BF16)
        out[at] = lax.dot_general(
            fold, summed, (((1,), (1,)), ((), ())), preferred_element_type=F32
        ).astype(BF16)
        return carry

    lax.fori_loop(0, out.shape[0], one_pair, 0, unroll=4)


def move(slots, occ, vir, blocks, own_slots):
    live_total, size, width = occ.shape
    wide = blocks.shape[2] // (own_slots * size) * width
    rows = blocks.shape[1]
    return pl.pallas_call(
        functools.partial(moved_kernel, own_slots),
        out_shape=jax.ShapeDtypeStruct((rows // size, wide // width * size, width), BF16),
        in_specs=[pl.BlockSpec(memory_space=pltpu.SMEM), VMEM, VMEM, VMEM],
        out_specs=VMEM,
        scratch_shapes=[pltpu.VMEM((live_total, rows, wide), BF16)],
        compiler_params=pltpu.CompilerParams(vmem_limit_bytes=40 * 2**20),
    )(slots, occ, vir, blocks)


def owned_rows(coefficient, names, group):
    local_blocks = coefficient.shape[0] // BS
    blocks = coefficient.reshape(local_blocks, BS, coefficient.shape[1])
    local_names = names - group * local_blocks
    owned = (local_names >= 0) & (local_names < local_blocks)
    picked = jnp.take(blocks, jnp.clip(local_names, 0, local_blocks - 1), axis=0)
    picked = jnp.where(owned[:, None, None], picked, jnp.zeros((), BF16))
    return picked.reshape(names.shape[0] * BS, coefficient.shape[1])


def own_gram(rows, energy, exponent_sign, tau_points, picks):
    factor = jnp.exp(exponent_sign * tau_points[:, None] * energy[None, :] / 2.0)
    scaled = (rows[None].astype(F32) * factor[:, None, :]).astype(BF16)
    own = jnp.concatenate(
        [lax.dynamic_slice_in_dim(scaled, pick * BS, BS, 1) for pick in picks], axis=1
    )
    return jnp.einsum("tin,tjn->tij", own, scaled, preferred_element_type=F32)


def per_device(groups, shards, c_occ, c_vir, e_occ, e_vir, tau_points, pair_blocks, block_count,
               three_center):
    own_slots = pair_blocks.shape[0]
    slot_total = own_slots * groups
    live_total = 5 * groups // 2
    group = lax.axis_index("pair")
    fields = 2 * own_slots + 1
    flat = jnp.concatenate([pair_blocks.reshape(-1), block_count])
    table = jnp.zeros((8, 128), jnp.int32).at[0, :fields].set(flat)
    tables = gather_table(table, groups)[:, 0, :fields]
    names = tables[:, :-1].reshape(slot_total, 2)
    counts = tables[:, -1]
    live = (jnp.arange(own_slots)[None, :] < counts[:, None]).reshape(slot_total)
    ids = jnp.arange(slot_total)
    ranks = jnp.sum(jnp.where(live[None, :] & (ids[None, :] < ids[:, None]), 1, 0), axis=1)
    select = live[None, :] & (ranks[None, :] == jnp.arange(live_total)[:, None])
    live_names = jnp.sum(jnp.where(select[:, :, None], names[None], 0), axis=1)
    rows = jnp.concatenate(
        [owned_rows(c_occ, live_names[:, 0], group), owned_rows(c_vir, live_names[:, 1], group)], axis=1
    )
    window = three_center[:WIN_DEV].reshape(PAIRS, WIN_DEV // PAIRS, own_slots, BS, BS)
    window = window.transpose(1, 4, 0, 2, 3).reshape(WIN_DEV // PAIRS * BS, PAIRS * own_slots * BS)
    rows, blocks, flat_blocks = sum_rows(rows, window, three_center, groups)
    before = jnp.sum(jnp.where(jnp.arange(groups) < group, counts, 0))
    picks = [jnp.minimum(before + k, live_total - 1) for k in range(own_slots)]
    n_occ = c_occ.shape[1]
    terms = jnp.concatenate(
        [
            own_gram(rows[:, :n_occ], e_occ, 1.0, tau_points, picks),
            own_gram(rows[:, n_occ:], e_vir, -1.0, tau_points, picks),
        ],
        axis=0,
    )
    tiles = sum_tiles(terms.reshape(2 * TAUS * own_slots * BS, live_total * BS), shards)
    width = TAUS * own_slots * BS
    live_ids = jnp.sum(jnp.where(select, ids[None, :], 0), axis=1)
    occ_tiles = tiles[:width].T.reshape(live_total, BS, width)
    moved = move(live_ids, occ_tiles, tiles[width:], blocks, own_slots)
    moved = moved.reshape(WIN_DEV // PAIRS, PAIRS, BS, TAUS, own_slots, BS)
    live_mask = jnp.arange(own_slots) < block_count[0]
    moved = jnp.where(live_mask[:, None], moved, jnp.zeros((), BF16))
    transformed = moved.transpose(3, 1, 0, 4, 2, 5).reshape(TAUS * WIN_DEV, own_slots * BS * BS)
    coupling = couple(flat_blocks, transformed, groups, shards)
    return coupling.reshape(coupling.shape[0], TAUS, shards * WIN_DEV)


def solution(mesh):
    placed = (
        P("pair", "aux"),
        P("pair", "aux"),
        P("aux"),
        P("aux"),
        P(),
        P("pair", None),
        P("pair"),
        P("aux", "pair", None),
    )
    return jax.shard_map(
        functools.partial(per_device, mesh.shape["pair"], mesh.shape["aux"]),
        mesh=mesh,
        in_specs=placed,
        out_specs=P(("aux", "pair"), None, None),
        check_vma=False,
    )
```

```python
import functools

import jax
import jax.numpy as jnp
from jax import lax
from jax.experimental import pallas as pl
from jax.experimental.pallas import tpu as pltpu
from jax.sharding import PartitionSpec as P

BS = 16
TAUS = 2
WIN_DEV = 128
PAIRS = 2
HOP = 2
MESH = pl.DeviceIdType.MESH
VMEM = pl.BlockSpec(memory_space=pltpu.VMEM)
DMA = pltpu.SemaphoreType.DMA
BF16 = jnp.bfloat16
F32 = jnp.float32


def params(collective_id):
    return pltpu.CompilerParams(
        collective_id=collective_id, has_side_effects=True, vmem_limit_bytes=40 * 2**20
    )


def greet(pair_peers, aux_peers=()):
    barrier = pltpu.get_barrier_semaphore()
    for peer in pair_peers:
        pl.semaphore_signal(barrier, inc=1, device_id={"pair": peer}, device_id_type=MESH)
    for peer in aux_peers:
        pl.semaphore_signal(barrier, inc=1, device_id={"aux": peer}, device_id_type=MESH)
    pl.semaphore_wait(barrier, len(pair_peers) + len(aux_peers))


def remote(source, target, send, received, axis, device):
    return pltpu.make_async_remote_copy(
        src_ref=source,
        dst_ref=target,
        send_sem=send,
        recv_sem=received,
        device_id={axis: device},
        device_id_type=MESH,
    )


def place():
    me = lax.axis_index("pair")
    core = lax.rem(me, 2)
    return me, core, me // 2, me + 1 - 2 * core


def table_kernel(groups, mine, out, send, received):
    me = lax.axis_index("pair")
    peers = [lax.rem(me + k, groups) for k in range(1, groups)]
    greet(peers)
    copies = []
    for k in range(groups - 1):
        copy = remote(mine, out.at[me], send.at[k], received.at[k], "pair", peers[k])
        copy.start()
        copies.append(copy)
    out[me] = mine[...]
    for copy in copies:
        copy.wait()


def gather_table(table, groups):
    return pl.pallas_call(
        functools.partial(table_kernel, groups),
        out_shape=jax.ShapeDtypeStruct((groups,) + table.shape, table.dtype),
        in_specs=[VMEM],
        out_specs=VMEM,
        scratch_shapes=[DMA((groups - 1,)), DMA((groups - 1,))],
        compiler_params=params(0),
    )(table)


def rows_kernel(chips, chunks, pieces, rows, window, whole, out, blocks, flat,
                own, right_in, left_in, right_out, left_out,
                own_send, own_recv, right_send, right_recv, left_send, left_recv,
                done_send, done_recv, far_send, far_recv, near_send, near_recv):
    me, core, chip, partner = place()
    last = chips - 1
    after = lax.rem(me + 2, 2 * chips)
    before = lax.rem(me + 2 * chips - 2, 2 * chips)
    line = [lax.rem(chip + k, chips) * 2 + core for k in range(1, chips)]
    greet([partner] + line)

    def swap(j):
        return remote(rows.at[1 - core, j], own.at[j], own_send.at[j], own_recv.at[j], "pair", partner)

    def rightward(j):
        return remote(right_out.at[j], right_in.at[j], right_send.at[j], right_recv.at[j], "pair", after)

    def leftward(j):
        return remote(left_out.at[j], left_in.at[j], left_send.at[j], left_recv.at[j], "pair", before)

    def finished(j):
        return remote(out.at[core, j], out.at[core, j], done_send.at[j], done_recv.at[j], "pair", partner)

    def start_swap(j, carry):
        swap(j).start()
        return carry

    lax.fori_loop(0, chunks, start_swap, 0)
    far = []
    for k, peer in enumerate(line):
        far.append(remote(window, blocks.at[me], far_send.at[k], far_recv.at[k], "pair", peer))
    near = [remote(window, blocks.at[me], near_send.at[0], near_recv.at[0], "pair", partner)]
    near[0].start()
    blocks[me] = window[...]

    def step(i, carry):
        @pl.when(i < pieces)
        def _():
            count, depth = whole.shape[0] // pieces, whole.shape[2]
            at = pl.ds(pl.multiple_of(i * count, BS), count)
            part = whole[at].astype(F32)
            for k in range(whole.shape[1]):
                flat[at, k * depth:(k + 1) * depth] = part[:, k, :].astype(flat.dtype)

        @pl.when(i < chunks)
        def _():
            swap(i).wait_recv()
            own[i] = own[i] + rows[core, i]

        to_right = i - HOP * chip

        @pl.when((to_right >= 0) & (to_right < chunks))
        def _():
            @pl.when(chip > 0)
            def _():
                rightward(to_right).wait_recv()

            @pl.when(chip == 0)
            def _():
                right_out[to_right] = own[to_right]

            @pl.when((chip > 0) & (chip < last))
            def _():
                right_out[to_right] = own[to_right] + right_in[to_right]

            @pl.when(chip < last)
            def _():
                rightward(to_right).start()

        to_left = i - HOP * (last - chip)

        @pl.when((to_left >= 0) & (to_left < chunks))
        def _():
            @pl.when(chip < last)
            def _():
                leftward(to_left).wait_recv()

            @pl.when(chip == last)
            def _():
                left_out[to_left] = own[to_left]

            @pl.when((chip > 0) & (chip < last))
            def _():
                left_out[to_left] = own[to_left] + left_in[to_left]

            @pl.when(chip > 0)
            def _():
                leftward(to_left).start()

        ready = i - HOP * jnp.maximum(chip, last - chip)

        @pl.when((ready >= 0) & (ready < chunks))
        def _():
            @pl.when(chip == 0)
            def _():
                out[core, ready] = own[ready] + left_in[ready]

            @pl.when(chip == last)
            def _():
                out[core, ready] = own[ready] + right_in[ready]

            @pl.when((chip > 0) & (chip < last))
            def _():
                out[core, ready] = own[ready] + left_in[ready] + right_in[ready]

            finished(ready).start()

        return carry

    lax.fori_loop(0, HOP * last, step, 0)
    for copy in far:
        copy.start()
    lax.fori_loop(HOP * last, chunks + HOP * last, step, 0)
    for k, copy in enumerate(far):
        copy.wait_recv()
        origin = lax.rem(chip + last - k, chips) * 2 + core
        pass_on = remote(
            blocks.at[origin], blocks.at[origin], near_send.at[k + 1], near_recv.at[k + 1], "pair", partner
        )
        pass_on.start()
        near.append(pass_on)

    def drain(j, carry):
        swap(j).wait_send()

        @pl.when(chip < last)
        def _():
            rightward(j).wait_send()

        @pl.when(chip > 0)
        def _():
            leftward(j).wait_send()

        finished(j).wait_send()
        remote(
            out.at[1 - core, j], out.at[1 - core, j], done_send.at[j], done_recv.at[j], "pair", partner
        ).wait_recv()
        return carry

    lax.fori_loop(0, chunks, drain, 0)
    for copy in near:
        copy.wait()
    for copy in far:
        copy.wait_send()


def sum_rows(rows, window, whole, groups):
    chunks = rows.shape[0] // (2 * BS)
    width = rows.shape[1]
    shape = (2, chunks, BS, width)
    chips = groups // 2
    units = whole.shape[0] // BS
    steps = chunks + HOP * (chips - 1)
    pieces = max(d for d in range(1, steps + 1) if units % d == 0)
    flat_shape = (whole.shape[0], whole.shape[1] * whole.shape[2])
    summed, blocks, flat = pl.pallas_call(
        functools.partial(rows_kernel, chips, chunks, pieces),
        out_shape=(
            jax.ShapeDtypeStruct(shape, rows.dtype),
            jax.ShapeDtypeStruct((groups,) + window.shape, window.dtype),
            jax.ShapeDtypeStruct(flat_shape, whole.dtype),
        ),
        in_specs=[VMEM, VMEM, VMEM],
        out_specs=(VMEM, VMEM, VMEM),
        scratch_shapes=[pltpu.VMEM(shape[1:], rows.dtype)] * 5
        + [DMA((chunks,))] * 8
        + [DMA((chips - 1,))] * 2
        + [DMA((chips,))] * 2,
        compiler_params=params(1),
    )(rows.reshape(shape), window, whole)
    return summed.reshape(rows.shape), blocks, flat


def tiles_kernel(shards, terms, tiles, held, term_send, term_recv, tile_send, tile_recv):
    shard = lax.axis_index("aux")
    peers = [flipped(shard, k, shards) for k in range(1, shards)]
    greet([], peers)
    parts = []
    for k, peer in enumerate(peers):
        copy = remote(terms.at[peer], held.at[k], term_send.at[k], term_recv.at[k], "aux", peer)
        copy.start()
        parts.append(copy)
    total = terms[shard]
    for k, copy in enumerate(parts):
        copy.wait_recv()
        total = total + held[k]
    tiles[shard] = total.astype(tiles.dtype)
    sums = []
    for k, peer in enumerate(peers):
        copy = remote(tiles.at[shard], tiles.at[shard], tile_send.at[k], tile_recv.at[k], "aux", peer)
        copy.start()
        sums.append(copy)
    for copy in sums:
        copy.wait()
    for copy in parts:
        copy.wait_send()


def sum_tiles(terms, shards):
    rows, width = terms.shape
    grouped = (shards, rows // shards, width)
    tiles = pl.pallas_call(
        functools.partial(tiles_kernel, shards),
        out_shape=jax.ShapeDtypeStruct(grouped, BF16),
        in_specs=[VMEM],
        out_specs=VMEM,
        scratch_shapes=[pltpu.VMEM((shards - 1,) + grouped[1:], F32)] + [DMA((shards - 1,))] * 4,
        compiler_params=params(2),
    )(terms.reshape(grouped))
    return tiles.reshape(rows, width)


def flipped(shard, k, shards):
    other, bit = 0, 1
    while bit < shards:
        other = other + lax.rem(shard // bit + k // bit, 2) * bit
        bit = bit * 2
    return other


def coupling_kernel(chips, shards, blocks, mine, out, kept, moved, near_out, near_in, leaving, arriving,
                    moved_send, moved_recv, near_send, near_recv, far_send, far_recv):
    me, core, chip, partner = place()
    shard = lax.axis_index("aux")
    last = chips - 1
    peers = [flipped(shard, k, shards) for k in range(1, shards)]
    greet([partner] + [lax.rem(chip + k, chips) * 2 + core for k in range(1, chips)], peers)

    def arrival(k):
        return remote(
            mine, moved.at[k], moved_send.at[k], moved_recv.at[k], "aux", flipped(shard, k, shards)
        )

    def target(j):
        return lax.rem(chip + 1 + j, chips)

    def swap(k, j):
        return remote(
            near_out.at[k, j], near_in.at[k, j], near_send.at[k, j], near_recv.at[k, j], "pair", partner
        )

    def hand_over(k, j):
        return remote(
            leaving.at[k, j], arriving.at[k, j], far_send.at[k, j], far_recv.at[k, j],
            "pair", target(j) * 2 + core,
        )

    for k in range(1, shards):
        arrival(k).start()
    moved[0] = mine[...]

    def product(j, to_core, right):
        left = blocks[target(j), to_core]
        return lax.dot_general(left, right, (((1,), (1,)), ((), ())), preferred_element_type=F32)

    def chunk(k, carry):
        @pl.when(k > 0)
        def _():
            arrival(k).wait_recv()

        def for_partner(j, carry):
            near_out[k, j] = product(j, 1 - core, moved[k]).astype(near_out.dtype)
            swap(k, j).start()
            return carry

        lax.fori_loop(0, chips, for_partner, 0)

        def for_line(j, carry):
            term = product(j, core, moved[k])
            swap(k, j).wait_recv()
            leaving[k, j] = (term + near_in[k, j].astype(F32)).astype(leaving.dtype)
            hand_over(k, j).start()
            return carry

        lax.fori_loop(0, last, for_line, 0)
        term = product(last, core, moved[k])
        swap(k, last).wait_recv()
        kept[k] = term + near_in[k, last].astype(F32)
        return carry

    lax.fori_loop(0, shards, chunk, 0)

    def collect(k, carry):
        total = kept[k]
        for j in range(last):
            hand_over(k, j).wait_recv()
            total = total + arriving[k, j].astype(F32)
        width = total.shape[1] // TAUS
        for t in range(TAUS):
            column = (t * shards + flipped(shard, k, shards)) * width
            out[:, pl.ds(pl.multiple_of(column, width), width)] = total[:, t * width:(t + 1) * width]
        for j in range(last):
            hand_over(k, j).wait_send()
        for j in range(chips):
            swap(k, j).wait_send()

        @pl.when(k > 0)
        def _():
            arrival(k).wait_send()

        return carry

    lax.fori_loop(0, shards, collect, 0)


def couple(blocks, moved, groups, shards):
    chips = groups // 2
    rows, depth = blocks.shape
    block = (rows // groups, moved.shape[0])
    return pl.pallas_call(
        functools.partial(coupling_kernel, chips, shards),
        out_shape=jax.ShapeDtypeStruct((block[0], shards * block[1]), F32),
        in_specs=[VMEM, VMEM],
        out_specs=VMEM,
        scratch_shapes=[
            pltpu.VMEM((shards,) + block, F32),
            pltpu.VMEM((shards,) + moved.shape, BF16),
            pltpu.VMEM((shards, chips) + block, BF16),
            pltpu.VMEM((shards, chips) + block, BF16),
            pltpu.VMEM((shards, chips - 1) + block, BF16),
            pltpu.VMEM((shards, chips - 1) + block, BF16),
        ]
        + [DMA((shards,))] * 2
        + [DMA((shards, chips))] * 2
        + [DMA((shards, chips - 1))] * 2,
        compiler_params=params(3),
    )(blocks.reshape(chips, 2, block[0], depth), moved)


def moved_kernel(own_slots, slots_ref, occ, vir, blocks, out, half, sums):
    live_total, size, width = occ.shape
    fold_rows = blocks.shape[2]
    pairs = fold_rows // (own_slots * size)
    wide = pairs * width
    rank = lax.broadcasted_iota(jnp.int32, (pairs * own_slots, size, wide), 0)
    side = lax.broadcasted_iota(jnp.int32, (pairs * own_slots, size, wide), 2) // width

    def one_slot(n, carry):
        slot = slots_ref[n]
        tile = occ[n].astype(F32)
        spread = jnp.concatenate([tile] * pairs, axis=1)[None]
        spread = jnp.where(rank == side * own_slots + lax.rem(slot, own_slots), spread, 0.0)
        spread = spread.reshape(fold_rows, wide).astype(BF16)
        half[n] = jnp.dot(
            blocks[slot // own_slots], spread, preferred_element_type=F32
        ).astype(BF16)
        return carry

    lax.fori_loop(0, live_total, one_slot, 0)
    row = lax.broadcasted_iota(jnp.int32, (width, wide), 0) // size
    column = lax.rem(lax.broadcasted_iota(jnp.int32, (width, wide), 1), width) // size
    same = row == column
    entry = lax.broadcasted_iota(jnp.int32, (pairs * size, wide), 0)
    lane = lax.broadcasted_iota(jnp.int32, (pairs * size, wide), 1)
    fold = jnp.where(entry == lane // width * size + lax.rem(lane, size), 1.0, 0.0).astype(BF16)

    def one_pair(at, carry):
        rows = pl.ds(pl.multiple_of(at * size, size), size)
        right = half[:, rows, :].reshape(live_total * size, wide)
        summed = jnp.dot(vir[...], right, preferred_element_type=F32)
        sums[at] = jnp.where(same, summed, 0.0).astype(BF16)
        return carry

    lax.fori_loop(0, out.shape[0], one_pair, 0, unroll=8)

    def one_fold(at, carry):
        out[at] = lax.dot_general(
            fold, sums[at], (((1,), (1,)), ((), ())), preferred_element_type=F32
        ).astype(BF16)
        return carry

    lax.fori_loop(0, out.shape[0], one_fold, 0, unroll=8)


def move(slots, occ, vir, blocks, own_slots):
    live_total, size, width = occ.shape
    wide = blocks.shape[2] // (own_slots * size) * width
    rows = blocks.shape[1]
    return pl.pallas_call(
        functools.partial(moved_kernel, own_slots),
        out_shape=jax.ShapeDtypeStruct((rows // size, wide // width * size, width), BF16),
        in_specs=[pl.BlockSpec(memory_space=pltpu.SMEM), VMEM, VMEM, VMEM],
        out_specs=VMEM,
        scratch_shapes=[
            pltpu.VMEM((live_total, rows, wide), BF16),
            pltpu.VMEM((rows // size, width, wide), BF16),
        ],
        compiler_params=pltpu.CompilerParams(vmem_limit_bytes=40 * 2**20),
    )(slots, occ, vir, blocks)


def pick_kernel(local_blocks, names, occ, vir, out, occ_sems, vir_sems):
    split = occ.shape[1]
    sides = ((occ, slice(0, split), occ_sems), (vir, slice(split, out.shape[1]), vir_sems))

    def each(act):
        def body(n, carry):
            rows = pl.ds(pl.multiple_of(n * BS, BS), BS)
            for side, (source, columns, sems) in enumerate(sides):
                name = names[side, n]
                owned = (name >= 0) & (name < local_blocks)
                block = jnp.clip(name, 0, local_blocks - 1)
                start = pl.multiple_of(block * BS, BS)
                copy = pltpu.make_async_copy(
                    source.at[pl.ds(start, BS), :], out.at[rows, columns], sems.at[n]
                )
                act(owned, copy, rows, columns)
            return carry

        lax.fori_loop(0, names.shape[1], body, 0)

    def begin(owned, copy, rows, columns):
        @pl.when(owned)
        def _():
            copy.start()

        @pl.when(jnp.logical_not(owned))
        def _():
            out[rows, columns] = jnp.zeros((BS, columns.stop - columns.start), out.dtype)

    def end(owned, copy, rows, columns):
        @pl.when(owned)
        def _():
            copy.wait()

    each(begin)
    each(end)


def pick_rows(names, c_occ, c_vir):
    count = names.shape[1]
    anywhere = pl.BlockSpec(memory_space=pl.ANY)
    return pl.pallas_call(
        functools.partial(pick_kernel, c_occ.shape[0] // BS),
        out_shape=jax.ShapeDtypeStruct((count * BS, c_occ.shape[1] + c_vir.shape[1]), c_occ.dtype),
        in_specs=[pl.BlockSpec(memory_space=pltpu.SMEM), anywhere, anywhere],
        out_specs=VMEM,
        scratch_shapes=[DMA((count,)), DMA((count,))],
        compiler_params=pltpu.CompilerParams(vmem_limit_bytes=40 * 2**20),
    )(names, c_occ, c_vir)


def own_gram(rows, energy, exponent_sign, tau_points, picks):
    factor = jnp.exp(exponent_sign * tau_points[:, None] * energy[None, :] / 2.0)
    scaled = (rows[None].astype(F32) * factor[:, None, :]).astype(BF16)
    own = jnp.concatenate(
        [lax.dynamic_slice_in_dim(scaled, pick * BS, BS, 1) for pick in picks], axis=1
    )
    return jnp.einsum("tin,tjn->tij", own, scaled, preferred_element_type=F32)


def per_device(groups, shards, c_occ, c_vir, e_occ, e_vir, tau_points, pair_blocks, block_count,
               three_center):
    own_slots = pair_blocks.shape[0]
    slot_total = own_slots * groups
    live_total = 5 * groups // 2
    group = lax.axis_index("pair")
    fields = 2 * own_slots + 1
    flat = jnp.concatenate([pair_blocks.reshape(-1), block_count])
    table = jnp.zeros((8, 128), jnp.int32).at[0, :fields].set(flat)
    tables = gather_table(table, groups)[:, 0, :fields]
    names = tables[:, :-1].reshape(slot_total, 2)
    counts = tables[:, -1]
    live = (jnp.arange(own_slots)[None, :] < counts[:, None]).reshape(slot_total)
    ids = jnp.arange(slot_total)
    ranks = jnp.sum(jnp.where(live[None, :] & (ids[None, :] < ids[:, None]), 1, 0), axis=1)
    select = live[None, :] & (ranks[None, :] == jnp.arange(live_total)[:, None])
    live_names = jnp.sum(jnp.where(select[:, :, None], names[None], 0), axis=1)
    rows = pick_rows(live_names.T - group * (c_occ.shape[0] // BS), c_occ, c_vir)
    window = three_center[:WIN_DEV].reshape(PAIRS, WIN_DEV // PAIRS, own_slots, BS, BS)
    window = window.transpose(1, 4, 0, 2, 3).reshape(WIN_DEV // PAIRS * BS, PAIRS * own_slots * BS)
    rows, blocks, flat_blocks = sum_rows(rows, window, three_center, groups)
    before = jnp.sum(jnp.where(jnp.arange(groups) < group, counts, 0))
    picks = [jnp.minimum(before + k, live_total - 1) for k in range(own_slots)]
    n_occ = c_occ.shape[1]
    terms = jnp.concatenate(
        [
            own_gram(rows[:, :n_occ], e_occ, 1.0, tau_points, picks),
            own_gram(rows[:, n_occ:], e_vir, -1.0, tau_points, picks),
        ],
        axis=0,
    )
    tiles = sum_tiles(terms.reshape(2 * TAUS * own_slots * BS, live_total * BS), shards)
    width = TAUS * own_slots * BS
    live_ids = jnp.sum(jnp.where(select, ids[None, :], 0), axis=1)
    occ_tiles = tiles[:width].T.reshape(live_total, BS, width)
    moved = move(live_ids, occ_tiles, tiles[width:], blocks, own_slots)
    moved = moved.reshape(WIN_DEV // PAIRS, PAIRS, BS, TAUS, own_slots, BS)
    live_mask = jnp.arange(own_slots) < block_count[0]
    moved = jnp.where(live_mask[:, None], moved, jnp.zeros((), BF16))
    transformed = moved.transpose(3, 1, 0, 4, 2, 5).reshape(TAUS * WIN_DEV, own_slots * BS * BS)
    coupling = couple(flat_blocks, transformed, groups, shards)
    return coupling.reshape(coupling.shape[0], TAUS, shards * WIN_DEV)


def solution(mesh):
    placed = (
        P("pair", "aux"),
        P("pair", "aux"),
        P("aux"),
        P("aux"),
        P(),
        P("pair", None),
        P("pair"),
        P("aux", "pair", None),
    )
    return jax.shard_map(
        functools.partial(per_device, mesh.shape["pair"], mesh.shape["aux"]),
        mesh=mesh,
        in_specs=placed,
        out_specs=P(("aux", "pair"), None, None),
        check_vma=False,
    )
```

```python
import functools

import jax
import jax.numpy as jnp
from jax import lax
from jax.experimental import pallas as pl
from jax.experimental.pallas import tpu as pltpu
from jax.sharding import PartitionSpec as P

BS = 16
TAUS = 2
WIN_DEV = 128
PAIRS = 2
HOP = 2
MESH = pl.DeviceIdType.MESH
VMEM = pl.BlockSpec(memory_space=pltpu.VMEM)
DMA = pltpu.SemaphoreType.DMA
BF16 = jnp.bfloat16
F32 = jnp.float32


def params(collective_id):
    return pltpu.CompilerParams(
        collective_id=collective_id, has_side_effects=True, vmem_limit_bytes=40 * 2**20
    )


def greet(pair_peers, aux_peers=()):
    barrier = pltpu.get_barrier_semaphore()
    for peer in pair_peers:
        pl.semaphore_signal(barrier, inc=1, device_id={"pair": peer}, device_id_type=MESH)
    for peer in aux_peers:
        pl.semaphore_signal(barrier, inc=1, device_id={"aux": peer}, device_id_type=MESH)
    pl.semaphore_wait(barrier, len(pair_peers) + len(aux_peers))


def remote(source, target, send, received, axis, device):
    return pltpu.make_async_remote_copy(
        src_ref=source,
        dst_ref=target,
        send_sem=send,
        recv_sem=received,
        device_id={axis: device},
        device_id_type=MESH,
    )


def place():
    me = lax.axis_index("pair")
    core = lax.rem(me, 2)
    return me, core, me // 2, me + 1 - 2 * core


def table_kernel(groups, mine, out, send, received):
    me = lax.axis_index("pair")
    peers = [lax.rem(me + k, groups) for k in range(1, groups)]
    greet(peers)
    copies = []
    for k in range(groups - 1):
        copy = remote(mine, out.at[me], send.at[k], received.at[k], "pair", peers[k])
        copy.start()
        copies.append(copy)
    out[me] = mine[...]
    for copy in copies:
        copy.wait()


def gather_table(table, groups):
    return pl.pallas_call(
        functools.partial(table_kernel, groups),
        out_shape=jax.ShapeDtypeStruct((groups,) + table.shape, table.dtype),
        in_specs=[VMEM],
        out_specs=VMEM,
        scratch_shapes=[DMA((groups - 1,)), DMA((groups - 1,))],
        compiler_params=params(0),
    )(table)


def rows_kernel(chips, chunks, pieces, rows, window, whole, out, blocks, flat,
                own, right_in, left_in, right_out, left_out,
                own_send, own_recv, right_send, right_recv, left_send, left_recv,
                done_send, done_recv, far_send, far_recv, near_send, near_recv):
    me, core, chip, partner = place()
    last = chips - 1
    after = lax.rem(me + 2, 2 * chips)
    before = lax.rem(me + 2 * chips - 2, 2 * chips)
    line = [lax.rem(chip + k, chips) * 2 + core for k in range(1, chips)]
    greet([partner] + line)

    def swap(j):
        return remote(rows.at[1 - core, j], own.at[j], own_send.at[j], own_recv.at[j], "pair", partner)

    def rightward(j):
        return remote(right_out.at[j], right_in.at[j], right_send.at[j], right_recv.at[j], "pair", after)

    def leftward(j):
        return remote(left_out.at[j], left_in.at[j], left_send.at[j], left_recv.at[j], "pair", before)

    def finished(j):
        return remote(out.at[core, j], out.at[core, j], done_send.at[j], done_recv.at[j], "pair", partner)

    def start_swap(j, carry):
        swap(j).start()
        return carry

    lax.fori_loop(0, chunks, start_swap, 0)
    far = []
    for k, peer in enumerate(line):
        far.append(remote(window, blocks.at[me], far_send.at[k], far_recv.at[k], "pair", peer))
    near = [remote(window, blocks.at[me], near_send.at[0], near_recv.at[0], "pair", partner)]
    near[0].start()
    blocks[me] = window[...]

    def step(i, carry):
        @pl.when(i < pieces)
        def _():
            count, depth = whole.shape[0] // pieces, whole.shape[2]
            at = pl.ds(pl.multiple_of(i * count, BS), count)
            part = whole[at].astype(F32)
            for k in range(whole.shape[1]):
                flat[at, k * depth:(k + 1) * depth] = part[:, k, :].astype(flat.dtype)

        @pl.when(i < chunks)
        def _():
            swap(i).wait_recv()
            own[i] = own[i] + rows[core, i]

        to_right = i - HOP * chip

        @pl.when((to_right >= 0) & (to_right < chunks))
        def _():
            @pl.when(chip > 0)
            def _():
                rightward(to_right).wait_recv()

            @pl.when(chip == 0)
            def _():
                right_out[to_right] = own[to_right]

            @pl.when((chip > 0) & (chip < last))
            def _():
                right_out[to_right] = own[to_right] + right_in[to_right]

            @pl.when(chip < last)
            def _():
                rightward(to_right).start()

        to_left = i - HOP * (last - chip)

        @pl.when((to_left >= 0) & (to_left < chunks))
        def _():
            @pl.when(chip < last)
            def _():
                leftward(to_left).wait_recv()

            @pl.when(chip == last)
            def _():
                left_out[to_left] = own[to_left]

            @pl.when((chip > 0) & (chip < last))
            def _():
                left_out[to_left] = own[to_left] + left_in[to_left]

            @pl.when(chip > 0)
            def _():
                leftward(to_left).start()

        ready = i - HOP * jnp.maximum(chip, last - chip)

        @pl.when((ready >= 0) & (ready < chunks))
        def _():
            @pl.when(chip == 0)
            def _():
                out[core, ready] = own[ready] + left_in[ready]

            @pl.when(chip == last)
            def _():
                out[core, ready] = own[ready] + right_in[ready]

            @pl.when((chip > 0) & (chip < last))
            def _():
                out[core, ready] = own[ready] + left_in[ready] + right_in[ready]

            finished(ready).start()

        return carry

    for copy in far:
        copy.start()
    lax.fori_loop(0, chunks + HOP * last, step, 0)
    for k, copy in enumerate(far):
        copy.wait_recv()
        origin = lax.rem(chip + last - k, chips) * 2 + core
        pass_on = remote(
            blocks.at[origin], blocks.at[origin], near_send.at[k + 1], near_recv.at[k + 1], "pair", partner
        )
        pass_on.start()
        near.append(pass_on)

    def drain(j, carry):
        swap(j).wait_send()

        @pl.when(chip < last)
        def _():
            rightward(j).wait_send()

        @pl.when(chip > 0)
        def _():
            leftward(j).wait_send()

        finished(j).wait_send()
        remote(
            out.at[1 - core, j], out.at[1 - core, j], done_send.at[j], done_recv.at[j], "pair", partner
        ).wait_recv()
        return carry

    lax.fori_loop(0, chunks, drain, 0)
    for copy in near:
        copy.wait()
    for copy in far:
        copy.wait_send()


def sum_rows(rows, window, whole, groups):
    chunks = rows.shape[0] // (2 * BS)
    width = rows.shape[1]
    shape = (2, chunks, BS, width)
    chips = groups // 2
    units = whole.shape[0] // BS
    steps = chunks + HOP * (chips - 1)
    pieces = max(d for d in range(1, steps + 1) if units % d == 0)
    flat_shape = (whole.shape[0], whole.shape[1] * whole.shape[2])
    summed, blocks, flat = pl.pallas_call(
        functools.partial(rows_kernel, chips, chunks, pieces),
        out_shape=(
            jax.ShapeDtypeStruct(shape, rows.dtype),
            jax.ShapeDtypeStruct((groups,) + window.shape, window.dtype),
            jax.ShapeDtypeStruct(flat_shape, whole.dtype),
        ),
        in_specs=[VMEM, VMEM, VMEM],
        out_specs=(VMEM, VMEM, VMEM),
        scratch_shapes=[pltpu.VMEM(shape[1:], rows.dtype)] * 5
        + [DMA((chunks,))] * 8
        + [DMA((chips - 1,))] * 2
        + [DMA((chips,))] * 2,
        compiler_params=params(1),
    )(rows.reshape(shape), window, whole)
    return summed.reshape(rows.shape), blocks, flat


def tiles_kernel(shards, terms, tiles, held, term_send, term_recv, tile_send, tile_recv):
    shard = lax.axis_index("aux")
    peers = [flipped(shard, k, shards) for k in range(1, shards)]
    greet([], peers)
    parts = []
    for k, peer in enumerate(peers):
        copy = remote(terms.at[peer], held.at[k], term_send.at[k], term_recv.at[k], "aux", peer)
        copy.start()
        parts.append(copy)
    total = terms[shard]
    for k, copy in enumerate(parts):
        copy.wait_recv()
        total = total + held[k]
    tiles[shard] = total.astype(tiles.dtype)
    sums = []
    for k, peer in enumerate(peers):
        copy = remote(tiles.at[shard], tiles.at[shard], tile_send.at[k], tile_recv.at[k], "aux", peer)
        copy.start()
        sums.append(copy)
    for copy in sums:
        copy.wait()
    for copy in parts:
        copy.wait_send()


def sum_tiles(terms, shards):
    rows, width = terms.shape
    grouped = (shards, rows // shards, width)
    tiles = pl.pallas_call(
        functools.partial(tiles_kernel, shards),
        out_shape=jax.ShapeDtypeStruct(grouped, BF16),
        in_specs=[VMEM],
        out_specs=VMEM,
        scratch_shapes=[pltpu.VMEM((shards - 1,) + grouped[1:], F32)] + [DMA((shards - 1,))] * 4,
        compiler_params=params(2),
    )(terms.reshape(grouped))
    return tiles.reshape(rows, width)


def flipped(shard, k, shards):
    other, bit = 0, 1
    while bit < shards:
        other = other + lax.rem(shard // bit + k // bit, 2) * bit
        bit = bit * 2
    return other


def coupling_kernel(chips, shards, blocks, mine, out, kept, moved, near_out, near_in, leaving, arriving,
                    moved_send, moved_recv, near_send, near_recv, far_send, far_recv):
    me, core, chip, partner = place()
    shard = lax.axis_index("aux")
    last = chips - 1
    peers = [flipped(shard, k, shards) for k in range(1, shards)]
    greet([partner] + [lax.rem(chip + k, chips) * 2 + core for k in range(1, chips)], peers)

    def arrival(k):
        return remote(
            mine, moved.at[k], moved_send.at[k], moved_recv.at[k], "aux", flipped(shard, k, shards)
        )

    def target(j):
        return lax.rem(chip + 1 + j, chips)

    def swap(k, j):
        return remote(
            near_out.at[k, j], near_in.at[k, j], near_send.at[k, j], near_recv.at[k, j], "pair", partner
        )

    def hand_over(k, j):
        return remote(
            leaving.at[k, j], arriving.at[k, j], far_send.at[k, j], far_recv.at[k, j],
            "pair", target(j) * 2 + core,
        )

    for k in range(1, shards):
        arrival(k).start()
    moved[0] = mine[...]

    def product(j, to_core, right):
        left = blocks[target(j), to_core]
        return lax.dot_general(left, right, (((1,), (1,)), ((), ())), preferred_element_type=F32)

    def chunk(k, carry):
        @pl.when(k > 0)
        def _():
            arrival(k).wait_recv()

        def for_partner(j, carry):
            near_out[k, j] = product(j, 1 - core, moved[k]).astype(near_out.dtype)
            swap(k, j).start()
            return carry

        lax.fori_loop(0, chips, for_partner, 0)

        def for_line(j, carry):
            term = product(j, core, moved[k])
            swap(k, j).wait_recv()
            leaving[k, j] = (term + near_in[k, j].astype(F32)).astype(leaving.dtype)
            hand_over(k, j).start()
            return carry

        lax.fori_loop(0, last, for_line, 0)
        term = product(last, core, moved[k])
        swap(k, last).wait_recv()
        kept[k] = term + near_in[k, last].astype(F32)
        return carry

    lax.fori_loop(0, shards, chunk, 0)

    def collect(k, carry):
        total = kept[k]
        for j in range(last):
            hand_over(k, j).wait_recv()
            total = total + arriving[k, j].astype(F32)
        width = total.shape[1] // TAUS
        for t in range(TAUS):
            column = (t * shards + flipped(shard, k, shards)) * width
            out[:, pl.ds(pl.multiple_of(column, width), width)] = total[:, t * width:(t + 1) * width]
        for j in range(last):
            hand_over(k, j).wait_send()
        for j in range(chips):
            swap(k, j).wait_send()

        @pl.when(k > 0)
        def _():
            arrival(k).wait_send()

        return carry

    lax.fori_loop(0, shards, collect, 0)


def couple(blocks, moved, groups, shards):
    chips = groups // 2
    rows, depth = blocks.shape
    block = (rows // groups, moved.shape[0])
    return pl.pallas_call(
        functools.partial(coupling_kernel, chips, shards),
        out_shape=jax.ShapeDtypeStruct((block[0], shards * block[1]), F32),
        in_specs=[VMEM, VMEM],
        out_specs=VMEM,
        scratch_shapes=[
            pltpu.VMEM((shards,) + block, F32),
            pltpu.VMEM((shards,) + moved.shape, BF16),
            pltpu.VMEM((shards, chips) + block, BF16),
            pltpu.VMEM((shards, chips) + block, BF16),
            pltpu.VMEM((shards, chips - 1) + block, BF16),
            pltpu.VMEM((shards, chips - 1) + block, BF16),
        ]
        + [DMA((shards,))] * 2
        + [DMA((shards, chips))] * 2
        + [DMA((shards, chips - 1))] * 2,
        compiler_params=params(3),
    )(blocks.reshape(chips, 2, block[0], depth), moved)


def moved_kernel(own_slots, slots_ref, occ, vir, blocks, out, half, sums):
    live_total, size, width = occ.shape
    fold_rows = blocks.shape[2]
    pairs = fold_rows // (own_slots * size)
    wide = pairs * width
    rank = lax.broadcasted_iota(jnp.int32, (pairs * own_slots, size, wide), 0)
    side = lax.broadcasted_iota(jnp.int32, (pairs * own_slots, size, wide), 2) // width

    def one_slot(n, carry):
        slot = slots_ref[n]
        tile = occ[n].astype(F32)
        spread = jnp.concatenate([tile] * pairs, axis=1)[None]
        spread = jnp.where(rank == side * own_slots + lax.rem(slot, own_slots), spread, 0.0)
        spread = spread.reshape(fold_rows, wide).astype(BF16)
        half[n] = jnp.dot(
            blocks[slot // own_slots], spread, preferred_element_type=F32
        ).astype(BF16)
        return carry

    lax.fori_loop(0, live_total, one_slot, 0)
    row = lax.broadcasted_iota(jnp.int32, (width, wide), 0) // size
    column = lax.rem(lax.broadcasted_iota(jnp.int32, (width, wide), 1), width) // size
    same = row == column
    entry = lax.broadcasted_iota(jnp.int32, (pairs * size, wide), 0)
    lane = lax.broadcasted_iota(jnp.int32, (pairs * size, wide), 1)
    fold = jnp.where(entry == lane // width * size + lax.rem(lane, size), 1.0, 0.0).astype(BF16)

    def one_pair(at, carry):
        rows = pl.ds(pl.multiple_of(at * size, size), size)
        right = half[:, rows, :].reshape(live_total * size, wide)
        summed = jnp.dot(vir[...], right, preferred_element_type=F32)
        sums[at] = jnp.where(same, summed, 0.0).astype(BF16)
        return carry

    lax.fori_loop(0, out.shape[0], one_pair, 0, unroll=8)

    def one_fold(at, carry):
        out[at] = lax.dot_general(
            fold, sums[at], (((1,), (1,)), ((), ())), preferred_element_type=F32
        ).astype(BF16)
        return carry

    lax.fori_loop(0, out.shape[0], one_fold, 0, unroll=8)


def move(slots, occ, vir, blocks, own_slots):
    live_total, size, width = occ.shape
    wide = blocks.shape[2] // (own_slots * size) * width
    rows = blocks.shape[1]
    return pl.pallas_call(
        functools.partial(moved_kernel, own_slots),
        out_shape=jax.ShapeDtypeStruct((rows // size, wide // width * size, width), BF16),
        in_specs=[pl.BlockSpec(memory_space=pltpu.SMEM), VMEM, VMEM, VMEM],
        out_specs=VMEM,
        scratch_shapes=[
            pltpu.VMEM((live_total, rows, wide), BF16),
            pltpu.VMEM((rows // size, width, wide), BF16),
        ],
        compiler_params=pltpu.CompilerParams(vmem_limit_bytes=40 * 2**20),
    )(slots, occ, vir, blocks)


def pick_kernel(local_blocks, names, occ, vir, out, occ_sems, vir_sems):
    split = occ.shape[1]
    sides = ((occ, slice(0, split), occ_sems), (vir, slice(split, out.shape[1]), vir_sems))

    def each(act):
        def body(n, carry):
            rows = pl.ds(pl.multiple_of(n * BS, BS), BS)
            for side, (source, columns, sems) in enumerate(sides):
                name = names[side, n]
                owned = (name >= 0) & (name < local_blocks)
                block = jnp.clip(name, 0, local_blocks - 1)
                start = pl.multiple_of(block * BS, BS)
                copy = pltpu.make_async_copy(
                    source.at[pl.ds(start, BS), :], out.at[rows, columns], sems.at[n]
                )
                act(owned, copy, rows, columns)
            return carry

        lax.fori_loop(0, names.shape[1], body, 0)

    def begin(owned, copy, rows, columns):
        @pl.when(owned)
        def _():
            copy.start()

        @pl.when(jnp.logical_not(owned))
        def _():
            out[rows, columns] = jnp.zeros((BS, columns.stop - columns.start), out.dtype)

    def end(owned, copy, rows, columns):
        @pl.when(owned)
        def _():
            copy.wait()

    each(begin)
    each(end)


def pick_rows(names, c_occ, c_vir):
    count = names.shape[1]
    anywhere = pl.BlockSpec(memory_space=pl.ANY)
    return pl.pallas_call(
        functools.partial(pick_kernel, c_occ.shape[0] // BS),
        out_shape=jax.ShapeDtypeStruct((count * BS, c_occ.shape[1] + c_vir.shape[1]), c_occ.dtype),
        in_specs=[pl.BlockSpec(memory_space=pltpu.SMEM), anywhere, anywhere],
        out_specs=VMEM,
        scratch_shapes=[DMA((count,)), DMA((count,))],
        compiler_params=pltpu.CompilerParams(vmem_limit_bytes=40 * 2**20),
    )(names, c_occ, c_vir)


def own_gram(rows, energy, exponent_sign, tau_points, picks):
    factor = jnp.exp(exponent_sign * tau_points[:, None] * energy[None, :] / 2.0)
    scaled = (rows[None].astype(F32) * factor[:, None, :]).astype(BF16)
    own = jnp.concatenate(
        [lax.dynamic_slice_in_dim(scaled, pick * BS, BS, 1) for pick in picks], axis=1
    )
    return jnp.einsum("tin,tjn->tij", own, scaled, preferred_element_type=F32)


def per_device(groups, shards, c_occ, c_vir, e_occ, e_vir, tau_points, pair_blocks, block_count,
               three_center):
    own_slots = pair_blocks.shape[0]
    slot_total = own_slots * groups
    live_total = 5 * groups // 2
    group = lax.axis_index("pair")
    fields = 2 * own_slots + 1
    flat = jnp.concatenate([pair_blocks.reshape(-1), block_count])
    table = jnp.zeros((8, 128), jnp.int32).at[0, :fields].set(flat)
    tables = gather_table(table, groups)[:, 0, :fields]
    names = tables[:, :-1].reshape(slot_total, 2)
    counts = tables[:, -1]
    live = (jnp.arange(own_slots)[None, :] < counts[:, None]).reshape(slot_total)
    ids = jnp.arange(slot_total)
    ranks = jnp.sum(jnp.where(live[None, :] & (ids[None, :] < ids[:, None]), 1, 0), axis=1)
    select = live[None, :] & (ranks[None, :] == jnp.arange(live_total)[:, None])
    live_names = jnp.sum(jnp.where(select[:, :, None], names[None], 0), axis=1)
    rows = pick_rows(live_names.T - group * (c_occ.shape[0] // BS), c_occ, c_vir)
    window = three_center[:WIN_DEV].reshape(PAIRS, WIN_DEV // PAIRS, own_slots, BS, BS)
    window = window.transpose(1, 4, 0, 2, 3).reshape(WIN_DEV // PAIRS * BS, PAIRS * own_slots * BS)
    rows, blocks, flat_blocks = sum_rows(rows, window, three_center, groups)
    before = jnp.sum(jnp.where(jnp.arange(groups) < group, counts, 0))
    picks = [jnp.minimum(before + k, live_total - 1) for k in range(own_slots)]
    n_occ = c_occ.shape[1]
    terms = jnp.concatenate(
        [
            own_gram(rows[:, :n_occ], e_occ, 1.0, tau_points, picks),
            own_gram(rows[:, n_occ:], e_vir, -1.0, tau_points, picks),
        ],
        axis=0,
    )
    tiles = sum_tiles(terms.reshape(2 * TAUS * own_slots * BS, live_total * BS), shards)
    width = TAUS * own_slots * BS
    live_ids = jnp.sum(jnp.where(select, ids[None, :], 0), axis=1)
    occ_tiles = tiles[:width].T.reshape(live_total, BS, width)
    moved = move(live_ids, occ_tiles, tiles[width:], blocks, own_slots)
    moved = moved.reshape(WIN_DEV // PAIRS, PAIRS, BS, TAUS, own_slots, BS)
    live_mask = jnp.arange(own_slots) < block_count[0]
    moved = jnp.where(live_mask[:, None], moved, jnp.zeros((), BF16))
    transformed = moved.transpose(3, 1, 0, 4, 2, 5).reshape(TAUS * WIN_DEV, own_slots * BS * BS)
    coupling = couple(flat_blocks, transformed, groups, shards)
    return coupling.reshape(coupling.shape[0], TAUS, shards * WIN_DEV)


def solution(mesh):
    placed = (
        P("pair", "aux"),
        P("pair", "aux"),
        P("aux"),
        P("aux"),
        P(),
        P("pair", None),
        P("pair"),
        P("aux", "pair", None),
    )
    return jax.shard_map(
        functools.partial(per_device, mesh.shape["pair"], mesh.shape["aux"]),
        mesh=mesh,
        in_specs=placed,
        out_specs=P(("aux", "pair"), None, None),
        check_vma=False,
    )
```
